256 devices in a mesh: row: 8 (over y, x_hi), col: 32 (over z, x_lo, core).
Axes of the slice: x: 4 (x_hi: 2, x_lo: 2; x = x_hi * 2 + x_lo), y: 4, z: 8, core: 2. Of those that a mesh axis runs over, the one named last changes fastest.
Arguments:
- fingerprints: bfloat16 [32768, 2048], P(('col', 'row')), may hold values from 0 to 4
- activity: bfloat16 [32768, 256], P(('col', 'row')), may hold values from -6 to 6
- label_mask: int32 [32768], P(('col', 'row')), may hold values 0 or 1
- pattern: int32 [64, 24], P('col'), may hold values from 0 to 63, as said below
- counts: int32 [64], P('col'), may hold values from 1 to 24
Outputs:
- labels: bfloat16 [32768, 256], P(('col', 'row'))
The draws below stay inside these ranges and needn't reach their ends.
Inputs may be any that keep to these rules, and one draw needn't show every extreme that they name: `pattern`: slot 0 of row block I holds I, and the 24 slots of one row block name distinct blocks.
All inputs are finite; a program needn't handle non-finite values. No bound on the sum of `label_mask` on one device may be relied on, other than what follows from the above.
Results may differ from the reference program's by a relative error of at most 0.0034.
Values may be sent and summed in bfloat16 or wider, within the bound.
No kernel may reach another device: no remote copies, remote signals or barrier semaphores. Data moves between devices by JAX's collectives and lax.ppermute only.
A program may use at most 128 MiB of HBM per device.

```python
import jax
import jax.numpy as jnp
from jax import lax

FP = 2048
TASKS = 256
BLK = 512
ITERS = 3
NCOMP = 32768
NBLK = 64
KMAX = 24


def pattern_parts(key):
    base_key = jax.random.fold_in(key, 11)
    order_key, first_key, second_key, pick_key = jax.random.split(base_key, 4)
    row_keys = jax.random.split(order_key, NBLK)
    others = jax.vmap(lambda row_key: jax.random.permutation(row_key, NBLK - 1))(row_keys).astype(jnp.int32)
    blocks = jnp.arange(NBLK, dtype=jnp.int32)[:, None]
    others = others + (others >= blocks).astype(jnp.int32)
    pattern = jnp.concatenate([blocks, others[:, :KMAX - 1]], axis=1)
    first_draw = jax.random.randint(first_key, (NBLK,), 0, KMAX)
    second_draw = jax.random.randint(second_key, (NBLK,), 0, KMAX)
    counts = 1 + first_draw * second_draw // KMAX
    chosen = jax.random.randint(pick_key, (), 0, NBLK)
    counts = jnp.where(jnp.arange(NBLK) == chosen, KMAX, counts).astype(jnp.int32)
    return (pattern, counts)


def draw_pattern(key, part):
    return pattern_parts(key)[0]


def draw_counts(key, part):
    return pattern_parts(key)[1]


def draw_fingerprints(key, part):
    present_key, value_key = jax.random.split(jax.random.fold_in(key, 5))
    present_mask = jax.random.bernoulli(present_key, 0.4, (NCOMP, FP))
    values = jax.random.uniform(value_key, (NCOMP, FP), jnp.float32, 0.5, 2.0)
    return jnp.where(present_mask, values, 0.0).astype(jnp.bfloat16)


def with_ends(result, rng, low, top_value):
    shape = result.shape
    place = [jax.random.randint(jax.random.fold_in(rng, axis), (), 0, shape[axis]) for axis in range(len(shape))]
    result = result.at[tuple(place)].set(low)
    longest = shape.index(max(shape))
    place[longest] = (place[longest] + 1) % shape[longest]
    return result.at[tuple(place)].set(top_value)


def steps_of(rng, shape, shards, least, high):
    gain = 1.0
    for position, blocks in shards:
        heights = jax.random.uniform(jax.random.fold_in(jax.random.fold_in(rng, 6), position), (blocks,), jnp.float32, least / len(shards), high / len(shards))
        gain = gain * jnp.repeat(jnp.exp(heights), shape[position] // blocks).reshape((-1,) + (1,) * (len(shape) - 1 - position))
    return gain


def centred(stream_key, extent, scale, most, pieces=(), kind=jnp.bfloat16):
    factor_of = steps_of(stream_key, extent, pieces, -0.22, 0.18) if pieces else 1.0
    result = jax.random.normal(stream_key, extent, jnp.float32) * scale * factor_of
    return jnp.minimum(jnp.maximum(result, -most), most).astype(kind)


def setup_inputs(seed: int = 0) -> dict:
    streams_of = jax.random.split(jax.random.key(seed), 6)
    fingerprints = draw_fingerprints(jax.random.fold_in(streams_of[5], 71), 0)
    activity = centred(streams_of[1], (NCOMP, TASKS), 1.0, 6.0, ((0, 256),))
    label_mask = with_ends((jax.random.randint(streams_of[2], (NCOMP,), 0, 10) < 3).astype(jnp.int32), jax.random.fold_in(streams_of[2], 1), 0, 1)
    pattern = draw_pattern(jax.random.fold_in(streams_of[5], 71), 0)
    counts = draw_counts(jax.random.fold_in(streams_of[5], 71), 0)
    return {"fingerprints": fingerprints, "activity": activity, "label_mask": label_mask, "pattern": pattern, "counts": counts}


WEIGHT_ROW = 0.6
WEIGHT_COL = 0.3
WEIGHT_SHARED = 0.1
SHARPNESS = 80.0
EPSILON = 1e-5
PROPAGATE = 0.8
ANCHOR = 0.2


def block_spread(fingerprints, squares, labels, pattern, counts, row_block):
    row_start = (row_block * BLK).astype(jnp.int32)
    row_prints = lax.dynamic_slice_in_dim(fingerprints, row_start, BLK, 0)
    row_squares = lax.dynamic_slice_in_dim(squares, row_start, BLK, 0)
    diagonal = jnp.eye(BLK, dtype=bool)

    def visit(running, column_slot):
        spread, degree = running
        col_block = pattern[row_block, column_slot]

        def active(unused):
            col_start = (col_block * BLK).astype(jnp.int32)
            col_prints = lax.dynamic_slice_in_dim(fingerprints, col_start, BLK, 0)
            col_squares = lax.dynamic_slice_in_dim(squares, col_start, BLK, 0)
            col_labels = lax.dynamic_slice_in_dim(labels, col_start, BLK, 0)
            inner = jnp.dot(row_prints, col_prints.T, preferred_element_type=jnp.float32)
            ratio = inner / (WEIGHT_ROW * row_squares[:, None] + WEIGHT_COL * col_squares[None, :] + WEIGHT_SHARED * inner + EPSILON)
            weights = jnp.exp(SHARPNESS * (ratio - 0.5))
            weights = jnp.where(diagonal & (col_block == row_block), 0.0, weights)
            return (spread + jnp.dot(weights.astype(jnp.bfloat16), col_labels, preferred_element_type=jnp.float32),
                    degree + jnp.sum(weights, axis=1))

        return lax.cond(column_slot < counts[row_block], active, lambda unused: (spread, degree), None), None

    start_state = (jnp.zeros((BLK, TASKS), jnp.float32), jnp.zeros((BLK,), jnp.float32))
    final_state, unused = lax.scan(visit, start_state, jnp.arange(KMAX, dtype=jnp.int32))
    return final_state


def reference(fingerprints, activity, label_mask, pattern, counts):
    squares = jnp.sum(jnp.square(fingerprints.astype(jnp.float32)), axis=1)
    seeded = activity.astype(jnp.float32) * label_mask.astype(jnp.float32)[:, None]
    labels = seeded.astype(jnp.bfloat16)
    all_blocks = jnp.arange(NBLK, dtype=jnp.int32)
    for iteration in range(ITERS):
        spread, degree = lax.map(lambda row_block: block_spread(fingerprints, squares, labels, pattern, counts, row_block), all_blocks)
        spread = spread.reshape(NCOMP, TASKS)
        degree = degree.reshape(NCOMP)
        labels = (PROPAGATE * spread / degree[:, None] + ANCHOR * seeded).astype(jnp.bfloat16)
    return labels
```

```python
import jax
import jax.numpy as jnp
from jax import lax
from jax.experimental import pallas as pl
from jax.experimental.pallas import tpu as pltpu
from jax.sharding import Mesh, PartitionSpec as P

ITERS = 3

WEIGHT_ROW = 0.6
WEIGHT_COL = 0.3
WEIGHT_SHARED = 0.1
SHARPNESS = 80.0
EPSILON = 1e-05
PROPAGATE = 0.8
ANCHOR = 0.2

AXES = ("y", "xh", "z", "xl", "core")
SIZES = (4, 2, 8, 2, 2)
LINE = ("core", "z")
PLANE = ("xl", "y", "xh")
PIECE = 128
ROWS = 16
BLOCKS = 4
WIDTH = 512
TILES = ROWS * BLOCKS
VMEM_LIMIT = 48 * 1024 * 1024


def weights_kernel(ids, meta, starts, rows, cols, row_sq, col_sq, weights, degree,
                   col_buf, row_buf, tile_buf, col_sem, row_sem, tile_sem):
    live = meta[0]
    own_tile = meta[1]
    own_offset = meta[2]

    def row_copy(t):
        slot = lax.rem(t, 3)
        return pltpu.make_async_copy(
            rows.at[lax.rem(ids[t], ROWS)], row_buf.at[slot], row_sem.at[slot]
        )

    def col_copy(j):
        return pltpu.make_async_copy(cols.at[j], col_buf.at[j], col_sem.at[j])

    def tile_copy(t):
        return pltpu.make_async_copy(
            tile_buf.at[ids[t]], weights.at[ids[t]], tile_sem.at[ids[t]]
        )

    col_copy(0).start()
    for first in range(2):
        @pl.when(first < live)
        def _():
            row_copy(first).start()
    for j in range(1, BLOCKS):
        col_copy(j).start()
    degree[...] = jnp.zeros_like(degree)
    gap = (
        lax.broadcasted_iota(jnp.int32, (PIECE, WIDTH), 1)
        - lax.broadcasted_iota(jnp.int32, (PIECE, WIDTH), 0)
    )

    def block(j, carry):
        col_copy(j).wait()

        def tile(t, inner_carry):
            @pl.when(t + 2 < live)
            def _():
                row_copy(t + 2).start()

            row_copy(t).wait()
            a = lax.rem(ids[t], ROWS)
            inner = lax.dot_general(
                row_buf[lax.rem(t, 3)], col_buf[j], (((1,), (1,)), ((), ())),
                preferred_element_type=jnp.float32,
            )
            ratio = inner / (
                WEIGHT_ROW * row_sq[a]
                + WEIGHT_COL * col_sq[j]
                + WEIGHT_SHARED * inner
                + EPSILON
            )
            offset = jnp.where(ids[t] == own_tile, own_offset, -2 * WIDTH)
            value = jnp.where(gap == offset, 0.0, jnp.exp(SHARPNESS * (ratio - 0.5)))
            tile_buf[ids[t]] = value.astype(jnp.bfloat16)
            tile_copy(t).start()
            degree[a] += (
                value[:, :128] + value[:, 128:256] + value[:, 256:384] + value[:, 384:]
            )
            return inner_carry

        return lax.fori_loop(starts[j], starts[j + 1], tile, carry)

    lax.fori_loop(0, BLOCKS, block, 0)

    def finish(t, carry):
        tile_copy(t).wait()
        return carry

    lax.fori_loop(0, live, finish, 0)


def build_weights(ids, meta, starts, rows, cols, row_sq, col_sq):
    smem = pl.BlockSpec(memory_space=pltpu.SMEM)
    vmem = pl.BlockSpec(memory_space=pltpu.VMEM)
    hbm = pl.BlockSpec(memory_space=pl.ANY)
    depth = rows.shape[-1]
    return pl.pallas_call(
        weights_kernel,
        out_shape=(
            jax.ShapeDtypeStruct((TILES, PIECE, WIDTH), jnp.bfloat16),
            jax.ShapeDtypeStruct((ROWS, PIECE, 128), jnp.float32),
        ),
        in_specs=[smem, smem, smem, hbm, hbm, vmem, vmem],
        out_specs=(hbm, vmem),
        scratch_shapes=[
            pltpu.VMEM((BLOCKS, WIDTH, depth), jnp.bfloat16),
            pltpu.VMEM((3, PIECE, depth), jnp.bfloat16),
            pltpu.VMEM((TILES, PIECE, WIDTH), jnp.bfloat16),
            pltpu.SemaphoreType.DMA((BLOCKS,)),
            pltpu.SemaphoreType.DMA((3,)),
            pltpu.SemaphoreType.DMA((TILES,)),
        ],
        compiler_params=pltpu.CompilerParams(vmem_limit_bytes=VMEM_LIMIT),
        name="weights",
    )(ids, meta, starts, rows, cols, row_sq, col_sq)


def spread_kernel(ids, meta, weights, labels, keep, send, total, tile_buf, tile_sem):
    live = meta[0]
    core = meta[3]
    half = ROWS // 2

    def tile_copy(t):
        return pltpu.make_async_copy(
            weights.at[ids[t]], tile_buf.at[ids[t]], tile_sem.at[ids[t]]
        )

    def begin(t, carry):
        tile_copy(t).start()
        return carry

    lax.fori_loop(0, live, begin, 0)
    total[...] = jnp.zeros_like(total)

    def tile(t, carry):
        tile_copy(t).wait()
        total[lax.rem(ids[t], ROWS)] += jnp.dot(
            tile_buf[ids[t]], labels[ids[t] // ROWS], preferred_element_type=jnp.float32
        )
        return carry

    lax.fori_loop(0, live, tile, 0)
    for piece in range(half):
        keep[piece] = total[core * half + piece]
        send[piece] = total[(1 - core) * half + piece].astype(jnp.bfloat16)


def spread_rows(ids, meta, weights, labels):
    smem = pl.BlockSpec(memory_space=pltpu.SMEM)
    vmem = pl.BlockSpec(memory_space=pltpu.VMEM)
    hbm = pl.BlockSpec(memory_space=pl.ANY)
    tasks = labels.shape[-1]
    return pl.pallas_call(
        spread_kernel,
        out_shape=(
            jax.ShapeDtypeStruct((ROWS // 2, PIECE, tasks), jnp.float32),
            jax.ShapeDtypeStruct((ROWS // 2, PIECE, tasks), jnp.bfloat16),
        ),
        in_specs=[smem, smem, hbm, vmem],
        out_specs=(vmem, vmem),
        scratch_shapes=[
            pltpu.VMEM((ROWS, PIECE, tasks), jnp.float32),
            pltpu.VMEM((TILES, PIECE, WIDTH), jnp.bfloat16),
            pltpu.SemaphoreType.DMA((TILES,)),
        ],
        compiler_params=pltpu.CompilerParams(vmem_limit_bytes=VMEM_LIMIT),
        name="spread",
    )(ids, meta, weights, labels)


def swap_cores(value):
    return lax.ppermute(value, "core", [(0, 1), (1, 0)])


def gather_labels(labels):
    copies = jnp.broadcast_to(labels[None], (ROWS,) + labels.shape)
    return lax.all_to_all(copies, PLANE, 0, 0).reshape(BLOCKS, WIDTH, labels.shape[1])


def body(fingerprints, activity, label_mask, pattern, counts):
    y, xh, z, xl, core = [lax.axis_index(axis) for axis in AXES]
    depth = fingerprints.shape[1]
    slots = pattern.shape[1]
    rows = lax.all_gather(fingerprints, LINE, axis=0, tiled=True).reshape(ROWS, PIECE, depth)
    cols = lax.all_gather(fingerprints, PLANE, axis=0, tiled=True).reshape(BLOCKS, WIDTH, depth)
    squares = jnp.sum(jnp.square(fingerprints.astype(jnp.float32)), axis=1)

    table = jnp.concatenate([counts[:, None], pattern], axis=1).astype(jnp.float32).reshape(-1)
    packed = jnp.concatenate([squares, table, jnp.zeros((PIECE - table.size,), jnp.float32)])
    line_info = lax.all_gather(packed, LINE, axis=0)
    row_sq = line_info[:, :PIECE].reshape(ROWS, PIECE, 1)
    tables = line_info[:, PIECE:PIECE + table.size].reshape(ROWS, 2, slots + 1).astype(jnp.int32)
    mine = lax.dynamic_index_in_dim(tables, y // 2, 1, keepdims=False)
    col_sq = lax.all_gather(squares, PLANE, axis=0, tiled=True).reshape(BLOCKS, 1, WIDTH)

    j = jnp.arange(BLOCKS, dtype=jnp.int32)
    col_block = (z * 4 + (j // 2) * 2 + core) * 2 + j % 2
    hit = (mine[None, :, 1:] == col_block[:, None, None]) & (
        jnp.arange(slots, dtype=jnp.int32)[None, None, :] < mine[None, :, :1]
    )
    live = jnp.any(hit, axis=2)
    flat = live.reshape(TILES).astype(jnp.int32)
    order = jnp.arange(TILES, dtype=jnp.int32)
    before = jnp.sum(jnp.where(order[None, :] < order[:, None], flat[None, :], 0), axis=1)
    ids = jnp.sum(
        jnp.where((before[None, :] == order[:, None]) & (flat[None, :] > 0), order[None, :], 0),
        axis=1,
    ).astype(jnp.int32)
    starts = jnp.sum(
        jnp.where(
            order[None, :] < (jnp.arange(8, dtype=jnp.int32) * ROWS)[:, None], flat[None, :], 0
        ),
        axis=1,
    ).astype(jnp.int32)
    own_tile = (xl * 2 + y // 2) * ROWS + core * 8 + z
    own_offset = ((y % 2) * 2 + xh) * PIECE
    meta = jnp.stack([jnp.sum(flat), own_tile, own_offset, core]).astype(jnp.int32)

    seeded = activity.astype(jnp.float32) * label_mask.astype(jnp.float32)[:, None]
    labels = seeded.astype(jnp.bfloat16)
    gathered = gather_labels(labels)
    weights, degree = build_weights(ids, meta, starts, rows, cols, row_sq, col_sq)

    degree = jnp.sum(degree, axis=2)
    degree_keep = lax.dynamic_slice_in_dim(degree, core * 8, 8, 0)
    degree_send = lax.dynamic_slice_in_dim(degree, (1 - core) * 8, 8, 0)
    degree_sum = degree_keep + swap_cores(degree_send)
    high = lax.reduce_precision(degree_sum, 8, 7)
    low = degree_sum - high
    degree_rows = jnp.concatenate([high, low], axis=1).astype(jnp.bfloat16)[:, None, :]
    degree_rows = jnp.concatenate(
        [degree_rows, jnp.zeros((8, 15, 2 * PIECE), jnp.bfloat16)], axis=1
    )

    for iteration in range(ITERS):
        keep, send = spread_rows(ids, meta, weights, gathered)
        part = (keep + swap_cores(send).astype(jnp.float32)).astype(jnp.bfloat16)
        if iteration == 0:
            part = jnp.concatenate([part, degree_rows], axis=1)
        parts = lax.all_to_all(part, "z", 0, 0)
        summed = jnp.sum(parts.astype(jnp.float32), axis=0)
        if iteration == 0:
            degree_own = summed[PIECE, :PIECE] + summed[PIECE, PIECE:]
            summed = summed[:PIECE]
        labels = (PROPAGATE * summed / degree_own[:, None] + ANCHOR * seeded).astype(jnp.bfloat16)
        if iteration < ITERS - 1:
            gathered = gather_labels(labels)
    return labels


def solution(mesh):
    split = Mesh(mesh.devices.reshape(SIZES), AXES)
    whole = ("z", "xl", "core", "y", "xh")
    blocks = ("z", "xl", "core")
    placed = (P(whole, None), P(whole, None), P(whole), P(blocks, None), P(blocks))
    return jax.shard_map(
        body, mesh=split, in_specs=placed, out_specs=P(whole, None), check_vma=False
    )
```

```python
import jax
import jax.numpy as jnp
from jax import lax
from jax.experimental import pallas as pl
from jax.experimental.pallas import tpu as pltpu
from jax.sharding import Mesh, PartitionSpec as P

ITERS = 3

WEIGHT_ROW = 0.6
WEIGHT_COL = 0.3
WEIGHT_SHARED = 0.1
SHARPNESS = 80.0
EPSILON = 1e-05
PROPAGATE = 0.8
ANCHOR = 0.2

AXES = ("y", "xh", "z", "xl", "core")
SIZES = (4, 2, 8, 2, 2)
PLANE = ("xl", "y", "xh")
PIECE = 128
ROWS = 16
BLOCKS = 4
WIDTH = 512
TILES = ROWS * BLOCKS
VMEM_LIMIT = 48 * 1024 * 1024


def weights_kernel(*refs):
    ids, meta, starts = refs[:3]
    rows = refs[3:3 + ROWS]
    (cols, row_sq, weights, degree, col_buf, row_buf, tile_buf, col_sq,
     col_sem, row_sem, tile_sem) = refs[3 + ROWS:]
    live = meta[0]
    own_offset = meta[1]
    own_tile = meta[2]

    def start_row(t):
        slot = lax.rem(t, 3)
        wanted = lax.rem(ids[t], ROWS)
        for a in range(ROWS):
            @pl.when(wanted == a)
            def _():
                pltpu.make_async_copy(
                    rows[a].at[pl.ds(0, PIECE)], row_buf.at[slot], row_sem.at[slot]
                ).start()

    def wait_row(t):
        slot = lax.rem(t, 3)
        pltpu.make_async_copy(
            rows[0].at[pl.ds(0, PIECE)], row_buf.at[slot], row_sem.at[slot]
        ).wait()

    def col_copy(j):
        return pltpu.make_async_copy(
            cols.at[j % 2, :, j // 2], col_buf.at[j], col_sem.at[j]
        )

    def tile_copy(t):
        return pltpu.make_async_copy(
            tile_buf.at[ids[t]], weights.at[ids[t]], tile_sem.at[ids[t]]
        )

    col_copy(0).start()
    for first in range(2):
        @pl.when(first < live)
        def _():
            start_row(first)
    for j in range(1, BLOCKS):
        col_copy(j).start()
    degree[...] = jnp.zeros_like(degree)
    gap = (
        lax.broadcasted_iota(jnp.int32, (PIECE, WIDTH), 1)
        - lax.broadcasted_iota(jnp.int32, (PIECE, WIDTH), 0)
    )
    depth = col_buf.shape[-1]
    ones = jnp.ones((8, 128), jnp.float32)

    def block(j, carry):
        pltpu.make_async_copy(cols.at[0, :, 0], col_buf.at[j], col_sem.at[j]).wait()

        @pl.when(starts[j] < starts[j + 1])
        def _():
            for sub in range(WIDTH // PIECE):
                partial = jnp.zeros((PIECE, 128), jnp.float32)
                for part in range(depth // 128):
                    values = col_buf[j, sub, :, part * 128:(part + 1) * 128].astype(jnp.float32)
                    partial += values * values
                col_sq[:, sub * PIECE:(sub + 1) * PIECE] = lax.dot_general(
                    ones, partial, (((1,), (1,)), ((), ())),
                    precision=lax.Precision.HIGHEST, preferred_element_type=jnp.float32,
                )

        def tile(t, inner_carry):
            @pl.when(t + 2 < live)
            def _():
                start_row(t + 2)

            wait_row(t)
            a = lax.rem(ids[t], ROWS)
            inner = lax.dot_general(
                row_buf[lax.rem(t, 3)], col_buf[j].reshape(WIDTH, depth),
                (((1,), (1,)), ((), ())),
                preferred_element_type=jnp.float32,
            )
            ratio = inner / (
                WEIGHT_ROW * row_sq[a]
                + WEIGHT_COL * col_sq[0:1, :]
                + WEIGHT_SHARED * inner
                + EPSILON
            )
            offset = jnp.where(ids[t] == own_tile, own_offset, -2 * WIDTH)
            value = jnp.where(gap == offset, 0.0, jnp.exp(SHARPNESS * (ratio - 0.5)))
            tile_buf[ids[t]] = value.astype(jnp.bfloat16)
            tile_copy(t).start()
            degree[a] += (
                value[:, :128] + value[:, 128:256] + value[:, 256:384] + value[:, 384:]
            )
            return inner_carry

        return lax.fori_loop(starts[j], starts[j + 1], tile, carry)

    lax.fori_loop(0, BLOCKS, block, 0)

    def finish(t, carry):
        tile_copy(t).wait()
        return carry

    lax.fori_loop(0, live, finish, 0)


def build_weights(ids, meta, starts, rows, cols, row_sq):
    smem = pl.BlockSpec(memory_space=pltpu.SMEM)
    vmem = pl.BlockSpec(memory_space=pltpu.VMEM)
    hbm = pl.BlockSpec(memory_space=pl.ANY)
    depth = cols.shape[-1]
    return pl.pallas_call(
        weights_kernel,
        out_shape=(
            jax.ShapeDtypeStruct((TILES, PIECE, WIDTH), jnp.bfloat16),
            jax.ShapeDtypeStruct((ROWS, PIECE, 128), jnp.float32),
        ),
        in_specs=[smem, smem, smem] + [hbm] * ROWS + [hbm, vmem],
        out_specs=(hbm, vmem),
        scratch_shapes=[
            pltpu.VMEM((BLOCKS, WIDTH // PIECE, PIECE, depth), jnp.bfloat16),
            pltpu.VMEM((3, PIECE, depth), jnp.bfloat16),
            pltpu.VMEM((TILES, PIECE, WIDTH), jnp.bfloat16),
            pltpu.VMEM((8, WIDTH), jnp.float32),
            pltpu.SemaphoreType.DMA((BLOCKS,)),
            pltpu.SemaphoreType.DMA((3,)),
            pltpu.SemaphoreType.DMA((TILES,)),
        ],
        compiler_params=pltpu.CompilerParams(vmem_limit_bytes=VMEM_LIMIT),
        cost_estimate=pl.CostEstimate(
            flops=16 * 2 * PIECE * WIDTH * depth,
            bytes_accessed=2 * (ROWS + 16) * PIECE * depth,
            transcendentals=16 * PIECE * WIDTH,
        ),
        name="weights",
    )(ids, meta, starts, *rows, cols, row_sq)


def spread_kernel(ids, meta, weights, labels, keep, send, total, tile_buf, tile_sem):
    live = meta[0]
    z = meta[3]
    half = ROWS // 2

    def tile_copy(t):
        return pltpu.make_async_copy(
            weights.at[ids[t]], tile_buf.at[ids[t]], tile_sem.at[ids[t]]
        )

    def begin(t, carry):
        tile_copy(t).start()
        return carry

    lax.fori_loop(0, live, begin, 0)
    total[...] = jnp.zeros_like(total)

    def tile(t, carry):
        tile_copy(t).wait()
        total[lax.rem(ids[t], ROWS)] += jnp.dot(
            tile_buf[ids[t]], labels[ids[t] // ROWS], preferred_element_type=jnp.float32
        )
        return carry

    lax.fori_loop(0, live, tile, 0)
    for piece in range(half):
        place = lax.rem(z - piece + half, half)
        keep[piece] = total[place]
        send[piece] = total[half + place].astype(jnp.bfloat16)


def spread_rows(ids, meta, weights, labels):
    smem = pl.BlockSpec(memory_space=pltpu.SMEM)
    vmem = pl.BlockSpec(memory_space=pltpu.VMEM)
    hbm = pl.BlockSpec(memory_space=pl.ANY)
    tasks = labels.shape[-1]
    return pl.pallas_call(
        spread_kernel,
        out_shape=(
            jax.ShapeDtypeStruct((ROWS // 2, PIECE, tasks), jnp.float32),
            jax.ShapeDtypeStruct((ROWS // 2, PIECE, tasks), jnp.bfloat16),
        ),
        in_specs=[smem, smem, hbm, vmem],
        out_specs=(vmem, vmem),
        scratch_shapes=[
            pltpu.VMEM((ROWS, PIECE, tasks), jnp.float32),
            pltpu.VMEM((TILES, PIECE, WIDTH), jnp.bfloat16),
            pltpu.SemaphoreType.DMA((TILES,)),
        ],
        compiler_params=pltpu.CompilerParams(vmem_limit_bytes=VMEM_LIMIT),
        name="spread",
    )(ids, meta, weights, labels)


def swap_cores(value):
    return lax.ppermute(value, "core", [(0, 1), (1, 0)])


def gather_labels(labels):
    copies = jnp.broadcast_to(labels[None], (ROWS,) + labels.shape)
    return lax.all_to_all(copies, PLANE, 0, 0).reshape(BLOCKS, WIDTH, labels.shape[1])


def body(fingerprints, activity, label_mask, pattern, counts):
    y, xh, z, xl, core = [lax.axis_index(axis) for axis in AXES]
    depth = fingerprints.shape[1]
    slots = pattern.shape[1]
    cols = lax.all_gather(fingerprints, ("y", "xh", "xl"), axis=0, tiled=True)
    cols = cols.reshape(2, 4, 2, PIECE, depth)

    squares = jnp.sum(jnp.square(fingerprints.astype(jnp.float32)), axis=1)
    square_high = lax.reduce_precision(squares, 8, 7)
    square_mid = lax.reduce_precision(squares - square_high, 8, 7)
    square_low = squares - square_high - square_mid
    table = jnp.concatenate([counts[:, None], pattern], axis=1).reshape(-1)
    info = jnp.concatenate([
        square_high, square_mid, square_low, table.astype(jnp.float32),
        jnp.zeros((depth - 3 * PIECE - table.size,), jnp.float32),
    ]).astype(jnp.bfloat16)
    extended = jnp.concatenate(
        [fingerprints, info[None], jnp.zeros((15, depth), jnp.bfloat16)], axis=0
    )
    upward = [extended]
    for step in range(4):
        upward.append(lax.ppermute(upward[-1], "z", [(i, (i + 1) % 8) for i in range(8)]))
    downward = [extended]
    for step in range(3):
        downward.append(lax.ppermute(downward[-1], "z", [(i, (i + 7) % 8) for i in range(8)]))
    rows = upward + [downward[3], downward[2], downward[1]]
    rows = rows + [swap_cores(row) for row in rows]
    line_info = jnp.stack([row[PIECE] for row in rows]).astype(jnp.float32)
    row_sq = (
        line_info[:, :PIECE] + line_info[:, PIECE:2 * PIECE] + line_info[:, 2 * PIECE:3 * PIECE]
    )[:, :, None]
    tables = line_info[:, 3 * PIECE:3 * PIECE + table.size].reshape(ROWS, 2, slots + 1)
    mine = lax.dynamic_index_in_dim(tables.astype(jnp.int32), y // 2, 1, keepdims=False)

    j = jnp.arange(BLOCKS, dtype=jnp.int32)
    col_block = (z * 4 + (j // 2) * 2 + core) * 2 + j % 2
    hit = (mine[None, :, 1:] == col_block[:, None, None]) & (
        jnp.arange(slots, dtype=jnp.int32)[None, None, :] < mine[None, :, :1]
    )
    live = jnp.any(hit, axis=2)
    flat = live.reshape(TILES).astype(jnp.int32)
    order = jnp.arange(TILES, dtype=jnp.int32)
    before = jnp.sum(jnp.where(order[None, :] < order[:, None], flat[None, :], 0), axis=1)
    ids = jnp.sum(
        jnp.where((before[None, :] == order[:, None]) & (flat[None, :] > 0), order[None, :], 0),
        axis=1,
    ).astype(jnp.int32)
    starts = jnp.sum(
        jnp.where(
            order[None, :] < (jnp.arange(8, dtype=jnp.int32) * ROWS)[:, None], flat[None, :], 0
        ),
        axis=1,
    ).astype(jnp.int32)
    own_tile = (xl * 2 + y // 2) * ROWS
    own_offset = ((y % 2) * 2 + xh) * PIECE
    meta = jnp.stack([jnp.sum(flat), own_offset, own_tile, z]).astype(jnp.int32)

    seeded = activity.astype(jnp.float32) * label_mask.astype(jnp.float32)[:, None]
    labels = seeded.astype(jnp.bfloat16)
    labels, cols = lax.optimization_barrier((labels, cols))
    gathered = gather_labels(labels)
    weights, degree = build_weights(ids, meta, starts, rows, cols, row_sq)

    degree = jnp.sum(degree, axis=2)
    places = (z - jnp.arange(8, dtype=jnp.int32)) % 8
    degree_sum = degree[:8][places] + swap_cores(degree[8:][places])
    high = lax.reduce_precision(degree_sum, 8, 7)
    low = degree_sum - high
    degree_rows = jnp.concatenate([high, low], axis=1).astype(jnp.bfloat16)[:, None, :]
    degree_rows = jnp.concatenate(
        [degree_rows, jnp.zeros((8, 15, 2 * PIECE), jnp.bfloat16)], axis=1
    )

    for iteration in range(ITERS):
        keep, send = spread_rows(ids, meta, weights, gathered)
        part = (keep + swap_cores(send).astype(jnp.float32)).astype(jnp.bfloat16)
        if iteration == 0:
            part = jnp.concatenate([part, degree_rows], axis=1)
        parts = lax.all_to_all(part, "z", 0, 0)
        summed = jnp.sum(parts.astype(jnp.float32), axis=0)
        if iteration == 0:
            degree_own = summed[PIECE, :PIECE] + summed[PIECE, PIECE:]
            summed = summed[:PIECE]
        labels = (PROPAGATE * summed / degree_own[:, None] + ANCHOR * seeded).astype(jnp.bfloat16)
        if iteration < ITERS - 1:
            gathered = gather_labels(labels)
    return labels


def solution(mesh):
    split = Mesh(mesh.devices.reshape(SIZES), AXES)
    whole = ("z", "xl", "core", "y", "xh")
    blocks = ("z", "xl", "core")
    placed = (P(whole, None), P(whole, None), P(whole), P(blocks, None), P(blocks))
    return jax.shard_map(
        body, mesh=split, in_specs=placed, out_specs=P(whole, None), check_vma=False
    )
```

```python
import jax
import jax.numpy as jnp
from jax import lax
from jax.experimental import pallas as pl
from jax.experimental.pallas import tpu as pltpu
from jax.sharding import Mesh, PartitionSpec as P

ITERS = 3

WEIGHT_ROW = 0.6
WEIGHT_COL = 0.3
WEIGHT_SHARED = 0.1
SHARPNESS = 80.0
EPSILON = 1e-05
PROPAGATE = 0.8
ANCHOR = 0.2

AXES = ("y", "xh", "z", "xl", "core")
SIZES = (4, 2, 8, 2, 2)
PLANE = ("xl", "y", "xh")
PIECE = 128
EXTRA = 16
ROWS = 16
BLOCKS = 4
WIDTH = 512
TILES = ROWS * BLOCKS
VMEM_LIMIT = 48 * 1024 * 1024


def weights_kernel(*refs):
    ids, meta, starts = refs[:3]
    rows = refs[3:3 + ROWS]
    (cols, row_sq, weights, keep, send, degree_keep, degree_send,
     col_buf, row_buf, tile_buf, label_raw, labels, total, degree, col_sq,
     col_sem, row_sem, tile_sem, label_sem) = refs[3 + ROWS:]
    live = meta[0]
    own_offset = meta[1]
    own_tile = meta[2]

    def start_row(t):
        slot = lax.rem(t, 3)
        wanted = lax.rem(ids[t], ROWS)
        for a in range(ROWS):
            @pl.when(wanted == a)
            def _():
                pltpu.make_async_copy(
                    rows[a], row_buf.at[slot], row_sem.at[slot]
                ).start()

    def wait_row(t):
        slot = lax.rem(t, 3)
        pltpu.make_async_copy(rows[0], row_buf.at[slot], row_sem.at[slot]).wait()

    def col_copy(j):
        return pltpu.make_async_copy(
            cols.at[j % 2, :, j // 2, pl.ds(0, PIECE)], col_buf.at[j], col_sem.at[j]
        )

    def tile_copy(t):
        return pltpu.make_async_copy(
            tile_buf.at[ids[t]], weights.at[ids[t]], tile_sem.at[ids[t]]
        )

    col_copy(0).start()
    for first in range(2):
        @pl.when(first < live)
        def _():
            start_row(first)
    label_copy = pltpu.make_async_copy(
        cols.at[:, :, :, pl.ds(PIECE, EXTRA)], label_raw, label_sem
    )
    label_copy.start()
    for j in range(1, BLOCKS):
        col_copy(j).start()
    degree[...] = jnp.zeros_like(degree)
    total[...] = jnp.zeros_like(total)
    label_copy.wait()
    tasks = labels.shape[-1]
    for j in range(BLOCKS):
        for sub in range(WIDTH // PIECE):
            for group in range(PIECE // EXTRA):
                first_row = sub * PIECE + group * EXTRA
                labels[j, first_row:first_row + EXTRA, :] = label_raw[
                    j % 2, sub, j // 2, :, group * tasks:(group + 1) * tasks
                ]
    gap = (
        lax.broadcasted_iota(jnp.int32, (PIECE, WIDTH), 1)
        - lax.broadcasted_iota(jnp.int32, (PIECE, WIDTH), 0)
    )
    depth = col_buf.shape[-1]
    ones = jnp.ones((8, 128), jnp.float32)

    def block(j, carry):
        pltpu.make_async_copy(
            cols.at[0, :, 0, pl.ds(0, PIECE)], col_buf.at[j], col_sem.at[j]
        ).wait()

        @pl.when(starts[j] < starts[j + 1])
        def _():
            for sub in range(WIDTH // PIECE):
                partial = jnp.zeros((PIECE, 128), jnp.float32)
                for part in range(depth // 128):
                    values = col_buf[j, sub, :, part * 128:(part + 1) * 128].astype(jnp.float32)
                    partial += values * values
                col_sq[:, sub * PIECE:(sub + 1) * PIECE] = lax.dot_general(
                    ones, partial, (((1,), (1,)), ((), ())),
                    precision=lax.Precision.HIGHEST, preferred_element_type=jnp.float32,
                )

        def tile(t, inner_carry):
            @pl.when(t + 2 < live)
            def _():
                start_row(t + 2)

            wait_row(t)
            a = lax.rem(ids[t], ROWS)
            inner = lax.dot_general(
                row_buf[lax.rem(t, 3)], col_buf[j].reshape(WIDTH, depth),
                (((1,), (1,)), ((), ())),
                preferred_element_type=jnp.float32,
            )
            ratio = inner / (
                WEIGHT_ROW * row_sq[a]
                + WEIGHT_COL * col_sq[0:1, :]
                + WEIGHT_SHARED * inner
                + EPSILON
            )
            offset = jnp.where(ids[t] == own_tile, own_offset, -2 * WIDTH)
            value = jnp.where(gap == offset, 0.0, jnp.exp(SHARPNESS * (ratio - 0.5)))
            half = value.astype(jnp.bfloat16)
            tile_buf[ids[t]] = half
            tile_copy(t).start()
            total[a] += jnp.dot(half, labels[j], preferred_element_type=jnp.float32)
            degree[a] += (
                value[:, :128] + value[:, 128:256] + value[:, 256:384] + value[:, 384:]
            )
            return inner_carry

        return lax.fori_loop(starts[j], starts[j + 1], tile, carry)

    lax.fori_loop(0, BLOCKS, block, 0)
    split_rows(meta[3], total, keep, send)
    half_rows = ROWS // 2
    for piece in range(half_rows):
        place = lax.rem(meta[3] - piece + half_rows, half_rows)
        for target, where in ((degree_keep, place), (degree_send, half_rows + place)):
            target[piece:piece + 1, :] = lax.dot_general(
                ones, degree[where], (((1,), (1,)), ((), ())),
                precision=lax.Precision.HIGHEST, preferred_element_type=jnp.float32,
            )[0:1, :]

    def finish(t, carry):
        tile_copy(t).wait()
        return carry

    lax.fori_loop(0, live, finish, 0)


def split_rows(z, total, keep, send):
    half = ROWS // 2
    for piece in range(half):
        place = lax.rem(z - piece + half, half)
        keep[piece] = total[place]
        send[piece] = total[half + place].astype(jnp.bfloat16)


def build_weights(ids, meta, starts, rows, cols, row_sq):
    smem = pl.BlockSpec(memory_space=pltpu.SMEM)
    vmem = pl.BlockSpec(memory_space=pltpu.VMEM)
    hbm = pl.BlockSpec(memory_space=pl.ANY)
    depth = cols.shape[-1]
    tasks = depth * EXTRA // PIECE
    return pl.pallas_call(
        weights_kernel,
        out_shape=(
            jax.ShapeDtypeStruct((TILES, PIECE, WIDTH), jnp.bfloat16),
            jax.ShapeDtypeStruct((ROWS // 2, PIECE, tasks), jnp.float32),
            jax.ShapeDtypeStruct((ROWS // 2, PIECE, tasks), jnp.bfloat16),
            jax.ShapeDtypeStruct((ROWS // 2, PIECE), jnp.float32),
            jax.ShapeDtypeStruct((ROWS // 2, PIECE), jnp.float32),
        ),
        in_specs=[smem, smem, smem] + [hbm] * ROWS + [hbm, vmem],
        out_specs=(hbm, vmem, vmem, vmem, vmem),
        scratch_shapes=[
            pltpu.VMEM((BLOCKS, WIDTH // PIECE, PIECE, depth), jnp.bfloat16),
            pltpu.VMEM((3, PIECE, depth), jnp.bfloat16),
            pltpu.VMEM((TILES, PIECE, WIDTH), jnp.bfloat16),
            pltpu.VMEM((2, 4, 2, EXTRA, depth), jnp.bfloat16),
            pltpu.VMEM((BLOCKS, WIDTH, tasks), jnp.bfloat16),
            pltpu.VMEM((ROWS, PIECE, tasks), jnp.float32),
            pltpu.VMEM((ROWS, PIECE, 128), jnp.float32),
            pltpu.VMEM((8, WIDTH), jnp.float32),
            pltpu.SemaphoreType.DMA((BLOCKS,)),
            pltpu.SemaphoreType.DMA((3,)),
            pltpu.SemaphoreType.DMA((TILES,)),
            pltpu.SemaphoreType.DMA,
        ],
        compiler_params=pltpu.CompilerParams(vmem_limit_bytes=VMEM_LIMIT),
        cost_estimate=pl.CostEstimate(
            flops=16 * 2 * PIECE * WIDTH * depth,
            bytes_accessed=2 * (ROWS + 16) * PIECE * depth,
            transcendentals=16 * PIECE * WIDTH,
        ),
        name="weights",
    )(ids, meta, starts, *rows, cols, row_sq)


def spread_kernel(ids, meta, weights, labels, keep, send, total, tile_buf, tile_sem):
    live = meta[0]

    def tile_copy(t):
        return pltpu.make_async_copy(
            weights.at[ids[t]], tile_buf.at[ids[t]], tile_sem.at[ids[t]]
        )

    def begin(t, carry):
        tile_copy(t).start()
        return carry

    lax.fori_loop(0, live, begin, 0)
    total[...] = jnp.zeros_like(total)

    def tile(t, carry):
        tile_copy(t).wait()
        total[lax.rem(ids[t], ROWS)] += jnp.dot(
            tile_buf[ids[t]], labels[ids[t] // ROWS], preferred_element_type=jnp.float32
        )
        return carry

    lax.fori_loop(0, live, tile, 0)
    split_rows(meta[3], total, keep, send)


def spread_rows(ids, meta, weights, labels):
    smem = pl.BlockSpec(memory_space=pltpu.SMEM)
    vmem = pl.BlockSpec(memory_space=pltpu.VMEM)
    hbm = pl.BlockSpec(memory_space=pl.ANY)
    tasks = labels.shape[-1]
    return pl.pallas_call(
        spread_kernel,
        out_shape=(
            jax.ShapeDtypeStruct((ROWS // 2, PIECE, tasks), jnp.float32),
            jax.ShapeDtypeStruct((ROWS // 2, PIECE, tasks), jnp.bfloat16),
        ),
        in_specs=[smem, smem, hbm, vmem],
        out_specs=(vmem, vmem),
        scratch_shapes=[
            pltpu.VMEM((ROWS, PIECE, tasks), jnp.float32),
            pltpu.VMEM((TILES, PIECE, WIDTH), jnp.bfloat16),
            pltpu.SemaphoreType.DMA((TILES,)),
        ],
        compiler_params=pltpu.CompilerParams(vmem_limit_bytes=VMEM_LIMIT),
        name="spread",
    )(ids, meta, weights, labels)


def swap_cores(value):
    return lax.ppermute(value, "core", [(0, 1), (1, 0)])


def gather_labels(labels):
    copies = jnp.broadcast_to(labels[None], (ROWS,) + labels.shape)
    return lax.all_to_all(copies, PLANE, 0, 0).reshape(BLOCKS, WIDTH, labels.shape[1])


def body(fingerprints, activity, label_mask, pattern, counts):
    y, xh, z, xl, core = [lax.axis_index(axis) for axis in AXES]
    depth = fingerprints.shape[1]
    slots = pattern.shape[1]
    tasks = activity.shape[1]
    seeded = activity.astype(jnp.float32) * label_mask.astype(jnp.float32)[:, None]
    labels = seeded.astype(jnp.bfloat16).reshape(PIECE // EXTRA, EXTRA, tasks)
    extended = jnp.concatenate(
        [fingerprints, labels.transpose(1, 0, 2).reshape(EXTRA, depth)], axis=0
    )
    cols = lax.all_gather(extended, ("y", "xh", "xl"), axis=0, tiled=True)
    cols = cols.reshape(2, 4, 2, PIECE + EXTRA, depth)

    upward = [fingerprints]
    for step in range(4):
        upward.append(lax.ppermute(upward[-1], "z", [(i, (i + 1) % 8) for i in range(8)]))
    downward = [fingerprints]
    for step in range(3):
        downward.append(lax.ppermute(downward[-1], "z", [(i, (i + 7) % 8) for i in range(8)]))
    rows = upward + [downward[3], downward[2], downward[1]]
    rows = rows + [swap_cores(row) for row in rows]

    squares = jnp.sum(jnp.square(fingerprints.astype(jnp.float32)), axis=1)
    table = jnp.concatenate([counts[:, None], pattern], axis=1).astype(jnp.float32).reshape(-1)
    info = jnp.concatenate([squares, table, jnp.zeros((PIECE - table.size,), jnp.float32)])
    info = jnp.broadcast_to(info[None, None], (ROWS, 8, 2 * PIECE))
    info = lax.all_to_all(info, ("core", "z"), 0, 0)[:, 0]
    away = jnp.arange(8, dtype=jnp.int32)
    nearby = (z - away) % 8
    line_info = info[jnp.concatenate([core * 8 + nearby, (1 - core) * 8 + nearby])]
    row_sq = line_info[:, :PIECE].reshape(ROWS, PIECE, 1)
    tables = line_info[:, PIECE:PIECE + table.size].reshape(ROWS, 2, slots + 1)
    mine = lax.dynamic_index_in_dim(tables.astype(jnp.int32), y // 2, 1, keepdims=False)

    j = jnp.arange(BLOCKS, dtype=jnp.int32)
    col_block = (z * 4 + (j // 2) * 2 + core) * 2 + j % 2
    hit = (mine[None, :, 1:] == col_block[:, None, None]) & (
        jnp.arange(slots, dtype=jnp.int32)[None, None, :] < mine[None, :, :1]
    )
    live = jnp.any(hit, axis=2)
    flat = live.reshape(TILES).astype(jnp.int32)
    order = jnp.arange(TILES, dtype=jnp.int32)
    before = jnp.sum(jnp.where(order[None, :] < order[:, None], flat[None, :], 0), axis=1)
    ids = jnp.sum(
        jnp.where((before[None, :] == order[:, None]) & (flat[None, :] > 0), order[None, :], 0),
        axis=1,
    ).astype(jnp.int32)
    starts = jnp.sum(
        jnp.where(
            order[None, :] < (jnp.arange(8, dtype=jnp.int32) * ROWS)[:, None], flat[None, :], 0
        ),
        axis=1,
    ).astype(jnp.int32)
    own_tile = (xl * 2 + y // 2) * ROWS
    own_offset = ((y % 2) * 2 + xh) * PIECE
    meta = jnp.stack([jnp.sum(flat), own_offset, own_tile, z]).astype(jnp.int32)

    weights, keep, send, degree_keep, degree_send = build_weights(
        ids, meta, starts, rows, cols, row_sq
    )
    degree_sum = degree_keep + swap_cores(degree_send)
    high = lax.reduce_precision(degree_sum, 8, 7)
    low = degree_sum - high
    degree_rows = jnp.concatenate([high, low], axis=1).astype(jnp.bfloat16)[:, None, :]
    degree_rows = jnp.concatenate(
        [degree_rows, jnp.zeros((8, 15, 2 * PIECE), jnp.bfloat16)], axis=1
    )

    for iteration in range(ITERS):
        if iteration > 0:
            keep, send = spread_rows(ids, meta, weights, gathered)
        part = (keep + swap_cores(send).astype(jnp.float32)).astype(jnp.bfloat16)
        if iteration == 0:
            part = jnp.concatenate([part, degree_rows], axis=1)
        parts = lax.all_to_all(part, "z", 0, 0)
        summed = jnp.sum(parts.astype(jnp.float32), axis=0)
        if iteration == 0:
            degree_own = summed[PIECE, :PIECE] + summed[PIECE, PIECE:]
            summed = summed[:PIECE]
        labels = (PROPAGATE * summed / degree_own[:, None] + ANCHOR * seeded).astype(jnp.bfloat16)
        if iteration < ITERS - 1:
            gathered = gather_labels(labels)
    return labels


def solution(mesh):
    split = Mesh(mesh.devices.reshape(SIZES), AXES)
    whole = ("z", "xl", "core", "y", "xh")
    blocks = ("z", "xl", "core")
    placed = (P(whole, None), P(whole, None), P(whole), P(blocks, None), P(blocks))
    return jax.shard_map(
        body, mesh=split, in_specs=placed, out_specs=P(whole, None), check_vma=False
    )
```

```python
import jax
import jax.numpy as jnp
from jax import lax
from jax.experimental import pallas as pl
from jax.experimental.pallas import tpu as pltpu
from jax.sharding import Mesh, PartitionSpec as P

ITERS = 3

WEIGHT_ROW = 0.6
WEIGHT_COL = 0.3
WEIGHT_SHARED = 0.1
SHARPNESS = 80.0
EPSILON = 1e-05
PROPAGATE = 0.8
ANCHOR = 0.2

AXES = ("y", "xh", "z", "xl", "core")
SIZES = (4, 2, 8, 2, 2)
PLANE = ("xl", "y", "xh")
PIECE = 128
EXTRA = 16
ROWS = 16
BLOCKS = 4
WIDTH = 512
TILES = ROWS * BLOCKS
VMEM_LIMIT = 48 * 1024 * 1024


def split_rows(z, total, keep, send):
    half = ROWS // 2
    for piece in range(half):
        place = lax.rem(z - piece + half, half)
        keep[piece] = total[place]
        send[piece] = total[half + place].astype(jnp.bfloat16)


def weights_kernel(pairs, meta, starts, rows, cols, row_sq, col_sq,
                   weights, keep, send, degree_keep, degree_send,
                   col_buf, row_buf, tile_buf, label_raw, labels, total, degree,
                   col_sem, row_sem, tile_sem, label_sem):
    live = starts[BLOCKS]
    own_offset = meta[1]
    own_tile = meta[2]
    z = meta[3]

    def row_copy(q, side):
        slot = lax.rem(q, 3)
        return pltpu.make_async_copy(
            rows.at[lax.rem(pairs[2 * q + side], ROWS)],
            row_buf.at[slot, pl.ds(side * PIECE, PIECE)],
            row_sem.at[slot, side],
        )

    def col_copy(j):
        return pltpu.make_async_copy(
            cols.at[j % 2, :, j // 2, pl.ds(0, PIECE)], col_buf.at[j], col_sem.at[j]
        )

    def tile_copy(tile_id):
        return pltpu.make_async_copy(
            tile_buf.at[tile_id], weights.at[tile_id], tile_sem.at[tile_id]
        )

    col_copy(0).start()
    for first in range(2):
        @pl.when(first < live)
        def _():
            row_copy(first, 0).start()
            row_copy(first, 1).start()
    label_copy = pltpu.make_async_copy(
        cols.at[:, :, :, pl.ds(PIECE, EXTRA)], label_raw, label_sem
    )
    label_copy.start()
    for j in range(1, BLOCKS):
        col_copy(j).start()
    degree[...] = jnp.zeros_like(degree)
    total[...] = jnp.zeros_like(total)
    label_copy.wait()
    for j in range(BLOCKS):
        for sub in range(WIDTH // PIECE):
            for group in range(labels.shape[1] // EXTRA):
                labels[
                    j, group * EXTRA:(group + 1) * EXTRA, sub * PIECE:(sub + 1) * PIECE
                ] = label_raw[j % 2, sub, j // 2, :, group * PIECE:(group + 1) * PIECE]
    lane = lax.broadcasted_iota(jnp.int32, (WIDTH, 2 * PIECE), 1)
    gap = jnp.where(
        lane < PIECE, lax.broadcasted_iota(jnp.int32, (WIDTH, 2 * PIECE), 0) - lane, -WIDTH
    )
    depth = col_buf.shape[-1]

    def block(j, carry):
        pltpu.make_async_copy(
            cols.at[0, :, 0, pl.ds(0, PIECE)], col_buf.at[j], col_sem.at[j]
        ).wait()

        def pair(q, inner_carry):
            @pl.when(q + 2 < live)
            def _():
                row_copy(q + 2, 0).start()
                row_copy(q + 2, 1).start()

            row_copy(q, 0).wait()
            row_copy(q, 1).wait()
            one = pairs[2 * q]
            two = pairs[2 * q + 1]
            place_one = lax.rem(one, ROWS)
            place_two = lax.rem(two, ROWS)
            inner = lax.dot_general(
                col_buf[j].reshape(WIDTH, depth), row_buf[lax.rem(q, 3)],
                (((1,), (1,)), ((), ())),
                preferred_element_type=jnp.float32,
            )
            row_part = jnp.concatenate([row_sq[place_one], row_sq[place_two]], axis=1)
            ratio = inner / (
                WEIGHT_ROW * row_part
                + WEIGHT_COL * col_sq[j]
                + WEIGHT_SHARED * inner
                + EPSILON
            )
            offset = jnp.where(one == own_tile, own_offset, -2 * WIDTH)
            value = jnp.where(gap == offset, 0.0, jnp.exp(SHARPNESS * (ratio - 0.5)))
            half = value.astype(jnp.bfloat16)
            spread = jnp.dot(labels[j], half, preferred_element_type=jnp.float32)
            sums = jnp.sum(value, axis=0, keepdims=True)
            tile_buf[one] = half[:, :PIECE]
            tile_copy(one).start()
            total[place_one] += spread[:, :PIECE]
            degree[pl.ds(place_one, 1), :] += sums[:, :PIECE]

            @pl.when(one != two)
            def _():
                tile_buf[two] = half[:, PIECE:]
                tile_copy(two).start()
                total[place_two] += spread[:, PIECE:]
                degree[pl.ds(place_two, 1), :] += sums[:, PIECE:]

            return inner_carry

        return lax.fori_loop(starts[j], starts[j + 1], pair, carry)

    lax.fori_loop(0, BLOCKS, block, 0)
    split_rows(z, total, keep, send)
    half_rows = ROWS // 2
    for piece in range(half_rows):
        place = lax.rem(z - piece + half_rows, half_rows)
        degree_keep[piece:piece + 1, :] = degree[pl.ds(place, 1), :]
        degree_send[piece:piece + 1, :] = degree[pl.ds(half_rows + place, 1), :]

    def finish(q, carry):
        tile_copy(pairs[2 * q]).wait()

        @pl.when(pairs[2 * q] != pairs[2 * q + 1])
        def _():
            tile_copy(pairs[2 * q + 1]).wait()

        return carry

    lax.fori_loop(0, live, finish, 0)


def build_weights(pairs, meta, starts, rows, cols, row_sq, col_sq):
    smem = pl.BlockSpec(memory_space=pltpu.SMEM)
    vmem = pl.BlockSpec(memory_space=pltpu.VMEM)
    hbm = pl.BlockSpec(memory_space=pl.ANY)
    depth = cols.shape[-1]
    tasks = depth * EXTRA // PIECE
    return pl.pallas_call(
        weights_kernel,
        out_shape=(
            jax.ShapeDtypeStruct((TILES, WIDTH, PIECE), jnp.bfloat16),
            jax.ShapeDtypeStruct((ROWS // 2, tasks, PIECE), jnp.float32),
            jax.ShapeDtypeStruct((ROWS // 2, tasks, PIECE), jnp.bfloat16),
            jax.ShapeDtypeStruct((ROWS // 2, PIECE), jnp.float32),
            jax.ShapeDtypeStruct((ROWS // 2, PIECE), jnp.float32),
        ),
        in_specs=[smem, smem, smem, hbm, hbm, vmem, vmem],
        out_specs=(hbm, vmem, vmem, vmem, vmem),
        scratch_shapes=[
            pltpu.VMEM((BLOCKS, WIDTH // PIECE, PIECE, depth), jnp.bfloat16),
            pltpu.VMEM((3, 2 * PIECE, depth), jnp.bfloat16),
            pltpu.VMEM((TILES, WIDTH, PIECE), jnp.bfloat16),
            pltpu.VMEM((2, 4, 2, EXTRA, depth), jnp.bfloat16),
            pltpu.VMEM((BLOCKS, tasks, WIDTH), jnp.bfloat16),
            pltpu.VMEM((ROWS, tasks, PIECE), jnp.float32),
            pltpu.VMEM((ROWS, PIECE), jnp.float32),
            pltpu.SemaphoreType.DMA((BLOCKS,)),
            pltpu.SemaphoreType.DMA((3, 2)),
            pltpu.SemaphoreType.DMA((TILES,)),
            pltpu.SemaphoreType.DMA,
        ],
        compiler_params=pltpu.CompilerParams(vmem_limit_bytes=VMEM_LIMIT),
        cost_estimate=pl.CostEstimate(
            flops=16 * 2 * PIECE * WIDTH * depth,
            bytes_accessed=2 * (ROWS + 16) * PIECE * depth,
            transcendentals=16 * PIECE * WIDTH,
        ),
        name="weights",
    )(pairs, meta, starts, rows, cols, row_sq, col_sq)


def spread_kernel(ids, meta, weights, pieces, keep, send, labels, total, tile_buf, tile_sem):
    live = meta[0]

    def tile_copy(t):
        return pltpu.make_async_copy(
            weights.at[ids[t]], tile_buf.at[ids[t]], tile_sem.at[ids[t]]
        )

    def begin(t, carry):
        tile_copy(t).start()
        return carry

    lax.fori_loop(0, live, begin, 0)
    total[...] = jnp.zeros_like(total)
    for j in range(BLOCKS):
        for sub in range(WIDTH // PIECE):
            labels[j, :, sub * PIECE:(sub + 1) * PIECE] = pieces[j * (WIDTH // PIECE) + sub]

    def tile(t, carry):
        tile_copy(t).wait()
        total[lax.rem(ids[t], ROWS)] += jnp.dot(
            labels[ids[t] // ROWS], tile_buf[ids[t]], preferred_element_type=jnp.float32
        )
        return carry

    lax.fori_loop(0, live, tile, 0)
    split_rows(meta[3], total, keep, send)


def spread_rows(ids, meta, weights, pieces):
    smem = pl.BlockSpec(memory_space=pltpu.SMEM)
    vmem = pl.BlockSpec(memory_space=pltpu.VMEM)
    hbm = pl.BlockSpec(memory_space=pl.ANY)
    tasks = pieces.shape[1]
    return pl.pallas_call(
        spread_kernel,
        out_shape=(
            jax.ShapeDtypeStruct((ROWS // 2, tasks, PIECE), jnp.float32),
            jax.ShapeDtypeStruct((ROWS // 2, tasks, PIECE), jnp.bfloat16),
        ),
        in_specs=[smem, smem, hbm, vmem],
        out_specs=(vmem, vmem),
        scratch_shapes=[
            pltpu.VMEM((BLOCKS, tasks, WIDTH), jnp.bfloat16),
            pltpu.VMEM((ROWS, tasks, PIECE), jnp.float32),
            pltpu.VMEM((TILES, WIDTH, PIECE), jnp.bfloat16),
            pltpu.SemaphoreType.DMA((TILES,)),
        ],
        compiler_params=pltpu.CompilerParams(vmem_limit_bytes=VMEM_LIMIT),
        name="spread",
    )(ids, meta, weights, pieces)


def swap_cores(value):
    return lax.ppermute(value, "core", [(0, 1), (1, 0)])


def gather_pieces(piece):
    copies = jnp.broadcast_to(piece[None], (ROWS,) + piece.shape)
    return lax.all_to_all(copies, PLANE, 0, 0)


def body(fingerprints, activity, label_mask, pattern, counts):
    y, xh, z, xl, core = [lax.axis_index(axis) for axis in AXES]
    depth = fingerprints.shape[1]
    slots = pattern.shape[1]
    tasks = activity.shape[1]
    seeded = activity.T.astype(jnp.float32) * label_mask.astype(jnp.float32)[None, :]
    labels = seeded.astype(jnp.bfloat16).reshape(tasks // EXTRA, EXTRA, PIECE)
    extended = jnp.concatenate(
        [fingerprints, labels.transpose(1, 0, 2).reshape(EXTRA, depth)], axis=0
    )
    cols = lax.all_gather(extended, ("y", "xh", "xl"), axis=0, tiled=True)
    cols = cols.reshape(2, 4, 2, PIECE + EXTRA, depth)

    upward = [fingerprints]
    for step in range(4):
        upward.append(lax.ppermute(upward[-1], "z", [(i, (i + 1) % 8) for i in range(8)]))
    downward = [fingerprints]
    for step in range(3):
        downward.append(lax.ppermute(downward[-1], "z", [(i, (i + 7) % 8) for i in range(8)]))
    rows = upward + [downward[3], downward[2], downward[1]]
    rows = jnp.stack(rows + [swap_cores(row) for row in rows])

    squares = jnp.sum(jnp.square(fingerprints.astype(jnp.float32)), axis=1)
    table = jnp.concatenate([counts[:, None], pattern], axis=1).astype(jnp.float32).reshape(-1)
    info = jnp.concatenate([squares, table, jnp.zeros((PIECE - table.size,), jnp.float32)])
    info = jnp.broadcast_to(info[None, None], (ROWS, 8, 2 * PIECE))
    info = lax.all_to_all(info, ("core", "z"), 0, 0)[:, 0]
    away = jnp.arange(8, dtype=jnp.int32)
    nearby = (z - away) % 8
    line_info = info[jnp.concatenate([core * 8 + nearby, (1 - core) * 8 + nearby])]
    row_sq = line_info[:, :PIECE].reshape(ROWS, 1, PIECE)
    col_sq = gather_pieces(jnp.broadcast_to(squares[None], (8, PIECE)))[:, 0]
    col_sq = col_sq.reshape(BLOCKS, WIDTH, 1)
    tables = line_info[:, PIECE:PIECE + table.size].reshape(ROWS, 2, slots + 1)
    mine = lax.dynamic_index_in_dim(tables.astype(jnp.int32), y // 2, 1, keepdims=False)

    j = jnp.arange(BLOCKS, dtype=jnp.int32)
    col_block = (z * 4 + (j // 2) * 2 + core) * 2 + j % 2
    hit = (mine[None, :, 1:] == col_block[:, None, None]) & (
        jnp.arange(slots, dtype=jnp.int32)[None, None, :] < mine[None, :, :1]
    )
    live = jnp.any(hit, axis=2)
    flat = live.reshape(TILES).astype(jnp.int32)
    order = jnp.arange(TILES, dtype=jnp.int32)
    before = jnp.sum(jnp.where(order[None, :] < order[:, None], flat[None, :], 0), axis=1)
    ids = jnp.sum(
        jnp.where((before[None, :] == order[:, None]) & (flat[None, :] > 0), order[None, :], 0),
        axis=1,
    ).astype(jnp.int32)
    counted = jnp.sum(live.astype(jnp.int32), axis=1)
    even = counted + counted % 2
    block_start = jnp.sum(jnp.where(j[None, :] < j[:, None], even[None, :], 0), axis=1)
    block_before = jnp.sum(jnp.where(j[None, :] < j[:, None], counted[None, :], 0), axis=1)
    position = before + jnp.repeat(block_start - block_before, ROWS)
    spot = jnp.arange(TILES + 8, dtype=jnp.int32)
    pairs = jnp.max(
        jnp.where((position[None, :] <= spot[:, None]) & (flat[None, :] > 0), order[None, :], 0),
        axis=1,
    ).astype(jnp.int32)
    starts = (jnp.concatenate([block_start, jnp.sum(even)[None]]) // 2).astype(jnp.int32)
    own_tile = (xl * 2 + y // 2) * ROWS
    own_offset = ((y % 2) * 2 + xh) * PIECE
    meta = jnp.stack([jnp.sum(flat), own_offset, own_tile, z]).astype(jnp.int32)

    weights, keep, send, degree_keep, degree_send = build_weights(
        pairs, meta, starts, rows, cols, row_sq, col_sq
    )
    degree_sum = degree_keep + swap_cores(degree_send)
    high = lax.reduce_precision(degree_sum, 8, 7)
    low = degree_sum - high
    degree_rows = jnp.stack([high, low], axis=1).astype(jnp.bfloat16)
    degree_rows = jnp.concatenate([degree_rows, jnp.zeros((8, 14, PIECE), jnp.bfloat16)], axis=1)

    for iteration in range(ITERS):
        if iteration > 0:
            keep, send = spread_rows(ids, meta, weights, gathered)
        part = (keep + swap_cores(send).astype(jnp.float32)).astype(jnp.bfloat16)
        if iteration == 0:
            part = jnp.concatenate([part, degree_rows], axis=1)
        parts = lax.all_to_all(part, "z", 0, 0)
        summed = jnp.sum(parts.astype(jnp.float32), axis=0)
        if iteration == 0:
            degree_own = summed[tasks] + summed[tasks + 1]
            summed = summed[:tasks]
        labels = (PROPAGATE * summed / degree_own[None, :] + ANCHOR * seeded).astype(jnp.bfloat16)
        if iteration < ITERS - 1:
            gathered = gather_pieces(labels)
    return labels.T


def solution(mesh):
    split = Mesh(mesh.devices.reshape(SIZES), AXES)
    whole = ("z", "xl", "core", "y", "xh")
    blocks = ("z", "xl", "core")
    placed = (P(whole, None), P(whole, None), P(whole), P(blocks, None), P(blocks))
    return jax.shard_map(
        body, mesh=split, in_specs=placed, out_specs=P(whole, None), check_vma=False
    )
```

```python
import jax
import jax.numpy as jnp
from jax import lax
from jax.experimental import pallas as pl
from jax.experimental.pallas import tpu as pltpu
from jax.sharding import Mesh, PartitionSpec as P

ITERS = 3

WEIGHT_ROW = 0.6
WEIGHT_COL = 0.3
WEIGHT_SHARED = 0.1
SHARPNESS = 80.0
EPSILON = 1e-05
PROPAGATE = 0.8
ANCHOR = 0.2

AXES = ("y", "xh", "z", "xl", "core")
SIZES = (4, 2, 8, 2, 2)
PLANE = ("xl", "y", "xh")
PIECE = 128
EXTRA = 16
ROWS = 16
BLOCKS = 4
WIDTH = 512
TILES = ROWS * BLOCKS
VMEM_LIMIT = 48 * 1024 * 1024


def split_rows(z, total, keep, send):
    half = ROWS // 2
    for piece in range(half):
        place = lax.rem(z - piece + half, half)
        keep[piece] = total[place]
        send[piece] = total[half + place].astype(jnp.bfloat16)


def weights_kernel(pairs, meta, starts, *refs):
    rows = refs[:ROWS]
    (cols, row_sq, col_sq, weights, keep, send, degree_keep, degree_send,
     col_buf, row_buf, tile_buf, label_raw, labels, total, degree,
     col_sem, row_sem, tile_sem, label_sem) = refs[ROWS:]
    live = starts[BLOCKS]
    own_offset = meta[1]
    own_tile = meta[2]
    z = meta[3]

    def row_copy(q, side, source):
        slot = lax.rem(q, 3)
        return pltpu.make_async_copy(
            rows[source], row_buf.at[slot, pl.ds(side * PIECE, PIECE)], row_sem.at[slot, side]
        )

    def start_rows(q):
        for side in range(2):
            wanted = lax.rem(pairs[2 * q + side], ROWS)
            for source in range(ROWS):
                @pl.when(wanted == source)
                def _():
                    row_copy(q, side, source).start()

    def col_copy(j):
        return pltpu.make_async_copy(
            cols.at[j % 2, :, j // 2, pl.ds(0, PIECE)], col_buf.at[j], col_sem.at[j]
        )

    def tile_copy(tile_id):
        return pltpu.make_async_copy(
            tile_buf.at[tile_id], weights.at[tile_id], tile_sem.at[tile_id]
        )

    col_copy(0).start()
    for first in range(2):
        @pl.when(first < live)
        def _():
            start_rows(first)
    label_copy = pltpu.make_async_copy(
        cols.at[:, :, :, pl.ds(PIECE, EXTRA)], label_raw, label_sem
    )
    label_copy.start()
    for j in range(1, BLOCKS):
        col_copy(j).start()
    degree[...] = jnp.zeros_like(degree)
    total[...] = jnp.zeros_like(total)
    label_copy.wait()
    for j in range(BLOCKS):
        for sub in range(WIDTH // PIECE):
            for group in range(labels.shape[1] // EXTRA):
                labels[
                    j, group * EXTRA:(group + 1) * EXTRA, sub * PIECE:(sub + 1) * PIECE
                ] = label_raw[j % 2, sub, j // 2, :, group * PIECE:(group + 1) * PIECE]
    lane = lax.broadcasted_iota(jnp.int32, (WIDTH, 2 * PIECE), 1)
    gap = jnp.where(
        lane < PIECE, lax.broadcasted_iota(jnp.int32, (WIDTH, 2 * PIECE), 0) - lane, -WIDTH
    )
    depth = col_buf.shape[-1]

    def block(j, carry):
        pltpu.make_async_copy(
            cols.at[0, :, 0, pl.ds(0, PIECE)], col_buf.at[j], col_sem.at[j]
        ).wait()

        def pair(q, inner_carry):
            @pl.when(q + 2 < live)
            def _():
                start_rows(q + 2)

            row_copy(q, 0, 0).wait()
            row_copy(q, 1, 0).wait()
            one = pairs[2 * q]
            two = pairs[2 * q + 1]
            place_one = lax.rem(one, ROWS)
            place_two = lax.rem(two, ROWS)
            inner = lax.dot_general(
                col_buf[j].reshape(WIDTH, depth), row_buf[lax.rem(q, 3)],
                (((1,), (1,)), ((), ())),
                preferred_element_type=jnp.float32,
            )
            row_part = jnp.concatenate([row_sq[place_one], row_sq[place_two]], axis=1)
            ratio = inner / (
                WEIGHT_ROW * row_part
                + WEIGHT_COL * col_sq[j]
                + WEIGHT_SHARED * inner
                + EPSILON
            )
            offset = jnp.where(one == own_tile, own_offset, -2 * WIDTH)
            value = jnp.where(gap == offset, 0.0, jnp.exp(SHARPNESS * (ratio - 0.5)))
            half = value.astype(jnp.bfloat16)
            spread = jnp.dot(labels[j], half, preferred_element_type=jnp.float32)
            sums = jnp.sum(value, axis=0, keepdims=True)
            tile_buf[one] = half[:, :PIECE]
            tile_copy(one).start()
            total[place_one] += spread[:, :PIECE]
            degree[pl.ds(place_one, 1), :] += sums[:, :PIECE]

            @pl.when(one != two)
            def _():
                tile_buf[two] = half[:, PIECE:]
                tile_copy(two).start()
                total[place_two] += spread[:, PIECE:]
                degree[pl.ds(place_two, 1), :] += sums[:, PIECE:]

            return inner_carry

        return lax.fori_loop(starts[j], starts[j + 1], pair, carry)

    lax.fori_loop(0, BLOCKS, block, 0)
    split_rows(z, total, keep, send)
    half_rows = ROWS // 2
    for piece in range(half_rows):
        place = lax.rem(z - piece + half_rows, half_rows)
        degree_keep[piece:piece + 1, :] = degree[pl.ds(place, 1), :]
        degree_send[piece:piece + 1, :] = degree[pl.ds(half_rows + place, 1), :]

    def finish(q, carry):
        tile_copy(pairs[2 * q]).wait()

        @pl.when(pairs[2 * q] != pairs[2 * q + 1])
        def _():
            tile_copy(pairs[2 * q + 1]).wait()

        return carry

    lax.fori_loop(0, live, finish, 0)


def build_weights(pairs, meta, starts, rows, cols, row_sq, col_sq):
    smem = pl.BlockSpec(memory_space=pltpu.SMEM)
    vmem = pl.BlockSpec(memory_space=pltpu.VMEM)
    hbm = pl.BlockSpec(memory_space=pl.ANY)
    depth = cols.shape[-1]
    tasks = depth * EXTRA // PIECE
    return pl.pallas_call(
        weights_kernel,
        out_shape=(
            jax.ShapeDtypeStruct((TILES, WIDTH, PIECE), jnp.bfloat16),
            jax.ShapeDtypeStruct((ROWS // 2, tasks, PIECE), jnp.float32),
            jax.ShapeDtypeStruct((ROWS // 2, tasks, PIECE), jnp.bfloat16),
            jax.ShapeDtypeStruct((ROWS // 2, PIECE), jnp.float32),
            jax.ShapeDtypeStruct((ROWS // 2, PIECE), jnp.float32),
        ),
        in_specs=[smem, smem, smem] + [hbm] * ROWS + [hbm, vmem, vmem],
        out_specs=(hbm, vmem, vmem, vmem, vmem),
        scratch_shapes=[
            pltpu.VMEM((BLOCKS, WIDTH // PIECE, PIECE, depth), jnp.bfloat16),
            pltpu.VMEM((3, 2 * PIECE, depth), jnp.bfloat16),
            pltpu.VMEM((TILES, WIDTH, PIECE), jnp.bfloat16),
            pltpu.VMEM((2, 4, 2, EXTRA, depth), jnp.bfloat16),
            pltpu.VMEM((BLOCKS, tasks, WIDTH), jnp.bfloat16),
            pltpu.VMEM((ROWS, tasks, PIECE), jnp.float32),
            pltpu.VMEM((ROWS, PIECE), jnp.float32),
            pltpu.SemaphoreType.DMA((BLOCKS,)),
            pltpu.SemaphoreType.DMA((3, 2)),
            pltpu.SemaphoreType.DMA((TILES,)),
            pltpu.SemaphoreType.DMA,
        ],
        compiler_params=pltpu.CompilerParams(vmem_limit_bytes=VMEM_LIMIT),
        cost_estimate=pl.CostEstimate(
            flops=16 * 2 * PIECE * WIDTH * depth,
            bytes_accessed=2 * (ROWS + 16) * PIECE * depth,
            transcendentals=16 * PIECE * WIDTH,
        ),
        name="weights",
    )(pairs, meta, starts, *rows, cols, row_sq, col_sq)


def spread_kernel(ids, meta, weights, pieces, keep, send, labels, total, tile_buf, tile_sem):
    live = meta[0]

    def tile_copy(t):
        return pltpu.make_async_copy(
            weights.at[ids[t]], tile_buf.at[ids[t]], tile_sem.at[ids[t]]
        )

    def begin(t, carry):
        tile_copy(t).start()
        return carry

    lax.fori_loop(0, live, begin, 0)
    total[...] = jnp.zeros_like(total)
    for j in range(BLOCKS):
        for sub in range(WIDTH // PIECE):
            labels[j, :, sub * PIECE:(sub + 1) * PIECE] = pieces[j * (WIDTH // PIECE) + sub]

    def tile(t, carry):
        tile_copy(t).wait()
        total[lax.rem(ids[t], ROWS)] += jnp.dot(
            labels[ids[t] // ROWS], tile_buf[ids[t]], preferred_element_type=jnp.float32
        )
        return carry

    lax.fori_loop(0, live, tile, 0)
    split_rows(meta[3], total, keep, send)


def spread_rows(ids, meta, weights, pieces):
    smem = pl.BlockSpec(memory_space=pltpu.SMEM)
    vmem = pl.BlockSpec(memory_space=pltpu.VMEM)
    hbm = pl.BlockSpec(memory_space=pl.ANY)
    tasks = pieces.shape[1]
    return pl.pallas_call(
        spread_kernel,
        out_shape=(
            jax.ShapeDtypeStruct((ROWS // 2, tasks, PIECE), jnp.float32),
            jax.ShapeDtypeStruct((ROWS // 2, tasks, PIECE), jnp.bfloat16),
        ),
        in_specs=[smem, smem, hbm, vmem],
        out_specs=(vmem, vmem),
        scratch_shapes=[
            pltpu.VMEM((BLOCKS, tasks, WIDTH), jnp.bfloat16),
            pltpu.VMEM((ROWS, tasks, PIECE), jnp.float32),
            pltpu.VMEM((TILES, WIDTH, PIECE), jnp.bfloat16),
            pltpu.SemaphoreType.DMA((TILES,)),
        ],
        compiler_params=pltpu.CompilerParams(vmem_limit_bytes=VMEM_LIMIT),
        name="spread",
    )(ids, meta, weights, pieces)


def swap_cores(value):
    return lax.ppermute(value, "core", [(0, 1), (1, 0)])


def gather_pieces(piece):
    copies = jnp.broadcast_to(piece[None], (ROWS,) + piece.shape)
    return lax.all_to_all(copies, PLANE, 0, 0)


def body(fingerprints, activity, label_mask, pattern, counts):
    y, xh, z, xl, core = [lax.axis_index(axis) for axis in AXES]
    depth = fingerprints.shape[1]
    slots = pattern.shape[1]
    tasks = activity.shape[1]
    seeded = activity.T.astype(jnp.float32) * label_mask.astype(jnp.float32)[None, :]
    labels = seeded.astype(jnp.bfloat16).reshape(tasks // EXTRA, EXTRA, PIECE)
    extended = jnp.concatenate(
        [fingerprints, labels.transpose(1, 0, 2).reshape(EXTRA, depth)], axis=0
    )
    cols = lax.all_gather(extended, ("y", "xh", "xl"), axis=0, tiled=True)
    cols = cols.reshape(2, 4, 2, PIECE + EXTRA, depth)

    upward = [fingerprints]
    for step in range(4):
        upward.append(lax.ppermute(upward[-1], "z", [(i, (i + 1) % 8) for i in range(8)]))
    downward = [fingerprints]
    for step in range(3):
        downward.append(lax.ppermute(downward[-1], "z", [(i, (i + 7) % 8) for i in range(8)]))
    rows = upward + [downward[3], downward[2], downward[1]]
    rows = rows + [swap_cores(row) for row in rows]

    squares = jnp.sum(jnp.square(fingerprints.astype(jnp.float32)), axis=1)
    table = jnp.concatenate([counts[:, None], pattern], axis=1).astype(jnp.float32).reshape(-1)
    info = jnp.concatenate([squares, table, jnp.zeros((PIECE - table.size,), jnp.float32)])
    info = jnp.broadcast_to(info[None, None], (ROWS, 8, 2 * PIECE))
    info = lax.all_to_all(info, ("core", "z"), 0, 0)[:, 0]
    away = jnp.arange(8, dtype=jnp.int32)
    nearby = (z - away) % 8
    line_info = info[jnp.concatenate([core * 8 + nearby, (1 - core) * 8 + nearby])]
    row_sq = line_info[:, :PIECE].reshape(ROWS, 1, PIECE)
    squares, rows[4], rows[5] = lax.optimization_barrier((squares, rows[4], rows[5]))
    col_sq = gather_pieces(jnp.broadcast_to(squares[None], (8, PIECE)))[:, 0]
    col_sq = col_sq.reshape(BLOCKS, WIDTH, 1)
    tables = line_info[:, PIECE:PIECE + table.size].reshape(ROWS, 2, slots + 1)
    mine = lax.dynamic_index_in_dim(tables.astype(jnp.int32), y // 2, 1, keepdims=False)

    j = jnp.arange(BLOCKS, dtype=jnp.int32)
    col_block = (z * 4 + (j // 2) * 2 + core) * 2 + j % 2
    hit = (mine[None, :, 1:] == col_block[:, None, None]) & (
        jnp.arange(slots, dtype=jnp.int32)[None, None, :] < mine[None, :, :1]
    )
    live = jnp.any(hit, axis=2)
    flat = live.reshape(TILES).astype(jnp.int32)
    order = jnp.arange(TILES, dtype=jnp.int32)
    before = jnp.sum(jnp.where(order[None, :] < order[:, None], flat[None, :], 0), axis=1)
    ids = jnp.sum(
        jnp.where((before[None, :] == order[:, None]) & (flat[None, :] > 0), order[None, :], 0),
        axis=1,
    ).astype(jnp.int32)
    counted = jnp.sum(live.astype(jnp.int32), axis=1)
    even = counted + counted % 2
    block_start = jnp.sum(jnp.where(j[None, :] < j[:, None], even[None, :], 0), axis=1)
    block_before = jnp.sum(jnp.where(j[None, :] < j[:, None], counted[None, :], 0), axis=1)
    position = before + jnp.repeat(block_start - block_before, ROWS)
    spot = jnp.arange(TILES + 8, dtype=jnp.int32)
    pairs = jnp.max(
        jnp.where((position[None, :] <= spot[:, None]) & (flat[None, :] > 0), order[None, :], 0),
        axis=1,
    ).astype(jnp.int32)
    starts = (jnp.concatenate([block_start, jnp.sum(even)[None]]) // 2).astype(jnp.int32)
    own_tile = (xl * 2 + y // 2) * ROWS
    own_offset = ((y % 2) * 2 + xh) * PIECE
    meta = jnp.stack([jnp.sum(flat), own_offset, own_tile, z]).astype(jnp.int32)

    weights, keep, send, degree_keep, degree_send = build_weights(
        pairs, meta, starts, rows, cols, row_sq, col_sq
    )
    degree_sum = degree_keep + swap_cores(degree_send)
    high = lax.reduce_precision(degree_sum, 8, 7)
    low = degree_sum - high
    degree_rows = jnp.stack([high, low], axis=1).astype(jnp.bfloat16)
    degree_rows = jnp.concatenate([degree_rows, jnp.zeros((8, 14, PIECE), jnp.bfloat16)], axis=1)

    for iteration in range(ITERS):
        if iteration > 0:
            keep, send = spread_rows(ids, meta, weights, gathered)
        part = (keep + swap_cores(send).astype(jnp.float32)).astype(jnp.bfloat16)
        if iteration == 0:
            part = jnp.concatenate([part, degree_rows], axis=1)
        parts = lax.all_to_all(part, "z", 0, 0)
        summed = jnp.sum(parts.astype(jnp.float32), axis=0)
        if iteration == 0:
            degree_own = summed[tasks] + summed[tasks + 1]
            summed = summed[:tasks]
        labels = (PROPAGATE * summed / degree_own[None, :] + ANCHOR * seeded).astype(jnp.bfloat16)
        if iteration < ITERS - 1:
            gathered = gather_pieces(labels)
    return labels.T


def solution(mesh):
    split = Mesh(mesh.devices.reshape(SIZES), AXES)
    whole = ("z", "xl", "core", "y", "xh")
    blocks = ("z", "xl", "core")
    placed = (P(whole, None), P(whole, None), P(whole), P(blocks, None), P(blocks))
    return jax.shard_map(
        body, mesh=split, in_specs=placed, out_specs=P(whole, None), check_vma=False
    )
```

```python
import jax
import jax.numpy as jnp
from jax import lax
from jax.experimental import pallas as pl
from jax.experimental.pallas import tpu as pltpu
from jax.sharding import Mesh, PartitionSpec as P

ITERS = 3

WEIGHT_ROW = 0.6
WEIGHT_COL = 0.3
WEIGHT_SHARED = 0.1
SHARPNESS = 80.0
EPSILON = 1e-05
PROPAGATE = 0.8
ANCHOR = 0.2

AXES = ("y", "xh", "z", "xl", "core")
SIZES = (4, 2, 8, 2, 2)
PLANE = ("xl", "y", "xh")
PIECE = 128
EXTRA = 16
ROWS = 16
BLOCKS = 4
WIDTH = 512
TILES = ROWS * BLOCKS
VMEM_LIMIT = 48 * 1024 * 1024


def split_rows(z, total, keep, send):
    half = ROWS // 2
    for piece in range(half):
        place = lax.rem(z - piece + half, half)
        keep[piece] = total[place]
        send[piece] = total[half + place].astype(jnp.bfloat16)


def weights_kernel(pairs, meta, starts, *refs):
    rows = refs[:ROWS]
    (cols, row_sq, col_sq, weights, keep, send, degree_keep, degree_send,
     col_buf, row_buf, tile_buf, label_raw, labels, total, degree,
     col_sem, row_sem, tile_sem, label_sem) = refs[ROWS:]
    live = starts[BLOCKS]
    own_offset = meta[1]
    own_tile = meta[2]
    z = meta[3]

    def row_copy(q, side, source):
        slot = lax.rem(q, 3)
        return pltpu.make_async_copy(
            rows[source], row_buf.at[slot, pl.ds(side * PIECE, PIECE)], row_sem.at[slot, side]
        )

    def start_rows(q):
        for side in range(2):
            wanted = lax.rem(pairs[2 * q + side], ROWS)
            for source in range(ROWS):
                @pl.when(wanted == source)
                def _():
                    row_copy(q, side, source).start()

    def col_copy(j):
        return pltpu.make_async_copy(
            cols.at[j % 2, :, j // 2, pl.ds(0, PIECE)], col_buf.at[j], col_sem.at[j]
        )

    def tile_copy(tile_id):
        return pltpu.make_async_copy(
            tile_buf.at[tile_id], weights.at[tile_id], tile_sem.at[tile_id]
        )

    col_copy(0).start()
    for first in range(2):
        @pl.when(first < live)
        def _():
            start_rows(first)
    label_copy = pltpu.make_async_copy(
        cols.at[:, :, :, pl.ds(PIECE, EXTRA)], label_raw, label_sem
    )
    label_copy.start()
    for j in range(1, BLOCKS):
        col_copy(j).start()
    degree[...] = jnp.zeros_like(degree)
    total[...] = jnp.zeros_like(total)
    label_copy.wait()
    for j in range(BLOCKS):
        for sub in range(WIDTH // PIECE):
            for group in range(labels.shape[1] // EXTRA):
                labels[
                    j, group * EXTRA:(group + 1) * EXTRA, sub * PIECE:(sub + 1) * PIECE
                ] = label_raw[j % 2, sub, j // 2, :, group * PIECE:(group + 1) * PIECE]
    lane = lax.broadcasted_iota(jnp.int32, (WIDTH, 2 * PIECE), 1)
    gap = jnp.where(
        lane < PIECE, lax.broadcasted_iota(jnp.int32, (WIDTH, 2 * PIECE), 0) - lane, -WIDTH
    )
    depth = col_buf.shape[-1]

    def block(j, carry):
        pltpu.make_async_copy(
            cols.at[0, :, 0, pl.ds(0, PIECE)], col_buf.at[j], col_sem.at[j]
        ).wait()

        def pair(q, inner_carry):
            @pl.when(q + 2 < live)
            def _():
                start_rows(q + 2)

            row_copy(q, 0, 0).wait()
            row_copy(q, 1, 0).wait()
            one = pairs[2 * q]
            two = pairs[2 * q + 1]
            place_one = lax.rem(one, ROWS)
            place_two = lax.rem(two, ROWS)
            inner = lax.dot_general(
                col_buf[j].reshape(WIDTH, depth), row_buf[lax.rem(q, 3)],
                (((1,), (1,)), ((), ())),
                preferred_element_type=jnp.float32,
            )
            row_part = jnp.concatenate([row_sq[place_one], row_sq[place_two]], axis=1)
            ratio = inner / (
                WEIGHT_ROW * row_part
                + WEIGHT_COL * col_sq[j]
                + WEIGHT_SHARED * inner
                + EPSILON
            )
            offset = jnp.where(one == own_tile, own_offset, -2 * WIDTH)
            value = jnp.where(gap == offset, 0.0, jnp.exp(SHARPNESS * (ratio - 0.5)))
            half = value.astype(jnp.bfloat16)
            spread = jnp.dot(labels[j], half, preferred_element_type=jnp.float32)
            sums = jnp.sum(value, axis=0, keepdims=True)
            tile_buf[one] = half[:, :PIECE]
            tile_copy(one).start()
            total[place_one] += spread[:, :PIECE]
            degree[pl.ds(place_one, 1), :] += sums[:, :PIECE]

            @pl.when(one != two)
            def _():
                tile_buf[two] = half[:, PIECE:]
                tile_copy(two).start()
                total[place_two] += spread[:, PIECE:]
                degree[pl.ds(place_two, 1), :] += sums[:, PIECE:]

            return inner_carry

        return lax.fori_loop(starts[j], starts[j + 1], pair, carry)

    lax.fori_loop(0, BLOCKS, block, 0)
    split_rows(z, total, keep, send)
    half_rows = ROWS // 2
    for piece in range(half_rows):
        place = lax.rem(z - piece + half_rows, half_rows)
        degree_keep[piece:piece + 1, :] = degree[pl.ds(place, 1), :]
        degree_send[piece:piece + 1, :] = degree[pl.ds(half_rows + place, 1), :]

    def finish(q, carry):
        tile_copy(pairs[2 * q]).wait()

        @pl.when(pairs[2 * q] != pairs[2 * q + 1])
        def _():
            tile_copy(pairs[2 * q + 1]).wait()

        return carry

    lax.fori_loop(0, live, finish, 0)


def build_weights(pairs, meta, starts, rows, cols, row_sq, col_sq):
    smem = pl.BlockSpec(memory_space=pltpu.SMEM)
    vmem = pl.BlockSpec(memory_space=pltpu.VMEM)
    hbm = pl.BlockSpec(memory_space=pl.ANY)
    depth = cols.shape[-1]
    tasks = depth * EXTRA // PIECE
    return pl.pallas_call(
        weights_kernel,
        out_shape=(
            jax.ShapeDtypeStruct((TILES, WIDTH, PIECE), jnp.bfloat16),
            jax.ShapeDtypeStruct((ROWS // 2, tasks, PIECE), jnp.float32),
            jax.ShapeDtypeStruct((ROWS // 2, tasks, PIECE), jnp.bfloat16),
            jax.ShapeDtypeStruct((ROWS // 2, PIECE), jnp.float32),
            jax.ShapeDtypeStruct((ROWS // 2, PIECE), jnp.float32),
        ),
        in_specs=[smem, smem, smem] + [hbm] * ROWS + [hbm, vmem, vmem],
        out_specs=(hbm, vmem, vmem, vmem, vmem),
        scratch_shapes=[
            pltpu.VMEM((BLOCKS, WIDTH // PIECE, PIECE, depth), jnp.bfloat16),
            pltpu.VMEM((3, 2 * PIECE, depth), jnp.bfloat16),
            pltpu.VMEM((TILES, WIDTH, PIECE), jnp.bfloat16),
            pltpu.VMEM((2, 4, 2, EXTRA, depth), jnp.bfloat16),
            pltpu.VMEM((BLOCKS, tasks, WIDTH), jnp.bfloat16),
            pltpu.VMEM((ROWS, tasks, PIECE), jnp.float32),
            pltpu.VMEM((ROWS, PIECE), jnp.float32),
            pltpu.SemaphoreType.DMA((BLOCKS,)),
            pltpu.SemaphoreType.DMA((3, 2)),
            pltpu.SemaphoreType.DMA((TILES,)),
            pltpu.SemaphoreType.DMA,
        ],
        compiler_params=pltpu.CompilerParams(vmem_limit_bytes=VMEM_LIMIT),
        cost_estimate=pl.CostEstimate(
            flops=16 * 2 * PIECE * WIDTH * depth,
            bytes_accessed=2 * (ROWS + 16) * PIECE * depth,
            transcendentals=16 * PIECE * WIDTH,
        ),
        name="weights",
    )(pairs, meta, starts, *rows, cols, row_sq, col_sq)


def spread_kernel(pairs, meta, starts, weights, *refs):
    shifted = refs[:4]
    keep, send, labels, total, tile_buf, tile_sem = refs[4:]
    live = starts[BLOCKS]
    z = meta[3]
    half = ROWS // 2

    def tile_copy(q, side):
        return pltpu.make_async_copy(
            weights.at[pairs[2 * q + side]],
            tile_buf.at[q, :, pl.ds(side * PIECE, PIECE)],
            tile_sem.at[q, side],
        )

    def begin(q, carry):
        tile_copy(q, 0).start()

        @pl.when(pairs[2 * q] != pairs[2 * q + 1])
        def _():
            tile_copy(q, 1).start()

        return carry

    lax.fori_loop(0, live, begin, 0)
    total[...] = jnp.zeros_like(total)
    for down in range(4):
        from_y = lax.rem(meta[4] - down + 4, 4)
        for right in range(4):
            from_x = lax.rem(meta[5] - right + 4, 4)
            block = lax.rem(from_x, 2) * 2 + from_y // 2
            sub = lax.rem(from_y, 2) * 2 + from_x // 2
            labels[block, sub] = shifted[down][right]

    def add(tile_id, value):
        a = lax.rem(tile_id, ROWS)
        side = a // half
        place = side * half + lax.rem(z - lax.rem(a, half) + half, half)
        total[place] += value

    def pair(q, carry):
        one = pairs[2 * q]
        two = pairs[2 * q + 1]
        tile_copy(q, 0).wait()

        @pl.when(one != two)
        def _():
            tile_copy(q, 1).wait()

        j = one // ROWS
        spread = jnp.dot(
            jnp.concatenate([labels[j, sub] for sub in range(WIDTH // PIECE)], axis=1),
            tile_buf[q], preferred_element_type=jnp.float32,
        )
        add(one, spread[:, :PIECE])

        @pl.when(one != two)
        def _():
            add(two, spread[:, PIECE:])

        return carry

    lax.fori_loop(0, live, pair, 0)
    keep[...] = total[:half]
    send[...] = total[half:].astype(jnp.bfloat16)


def spread_rows(pairs, meta, starts, weights, shifted):
    smem = pl.BlockSpec(memory_space=pltpu.SMEM)
    vmem = pl.BlockSpec(memory_space=pltpu.VMEM)
    hbm = pl.BlockSpec(memory_space=pl.ANY)
    tasks = shifted[0].shape[1]
    return pl.pallas_call(
        spread_kernel,
        out_shape=(
            jax.ShapeDtypeStruct((ROWS // 2, tasks, PIECE), jnp.float32),
            jax.ShapeDtypeStruct((ROWS // 2, tasks, PIECE), jnp.bfloat16),
        ),
        in_specs=[smem, smem, smem, hbm] + [vmem] * 4,
        out_specs=(vmem, vmem),
        scratch_shapes=[
            pltpu.VMEM((BLOCKS, WIDTH // PIECE, tasks, PIECE), jnp.bfloat16),
            pltpu.VMEM((ROWS, tasks, PIECE), jnp.float32),
            pltpu.VMEM((TILES // 2, WIDTH, 2 * PIECE), jnp.bfloat16),
            pltpu.SemaphoreType.DMA((TILES // 2, 2)),
        ],
        compiler_params=pltpu.CompilerParams(vmem_limit_bytes=VMEM_LIMIT),
        name="spread",
    )(pairs, meta, starts, weights, *shifted)


def swap_cores(value):
    return lax.ppermute(value, "core", [(0, 1), (1, 0)])


def gather_pieces(piece):
    copies = jnp.broadcast_to(piece[None], (ROWS,) + piece.shape)
    return lax.all_to_all(copies, PLANE, 0, 0)


def shift_plane(value, down, right):
    moves = [
        (y * 4 + x, (y + down) % 4 * 4 + (x + right) % 4) for y in range(4) for x in range(4)
    ]
    return lax.ppermute(value, ("y", "xh", "xl"), moves)


def gather_shifted(labels):
    one, three, two = [shift_plane(labels, 0, right) for right in (1, 3, 2)]
    line = jnp.stack([labels, one, two, three])
    one, three, two = [shift_plane(line, down, 0) for down in (1, 3, 2)]
    return [line, one, two, three]


def body(fingerprints, activity, label_mask, pattern, counts):
    y, xh, z, xl, core = [lax.axis_index(axis) for axis in AXES]
    depth = fingerprints.shape[1]
    slots = pattern.shape[1]
    tasks = activity.shape[1]
    seeded = activity.T.astype(jnp.float32) * label_mask.astype(jnp.float32)[None, :]
    labels = seeded.astype(jnp.bfloat16).reshape(tasks // EXTRA, EXTRA, PIECE)
    extended = jnp.concatenate(
        [fingerprints, labels.transpose(1, 0, 2).reshape(EXTRA, depth)], axis=0
    )
    cols = lax.all_gather(extended, ("y", "xh", "xl"), axis=0, tiled=True)
    cols = cols.reshape(2, 4, 2, PIECE + EXTRA, depth)

    upward = [fingerprints]
    for step in range(4):
        upward.append(lax.ppermute(upward[-1], "z", [(i, (i + 1) % 8) for i in range(8)]))
    downward = [fingerprints]
    for step in range(3):
        downward.append(lax.ppermute(downward[-1], "z", [(i, (i + 7) % 8) for i in range(8)]))
    rows = upward + [downward[3], downward[2], downward[1]]
    rows = rows + [swap_cores(row) for row in rows]

    squares = jnp.sum(jnp.square(fingerprints.astype(jnp.float32)), axis=1)
    table = jnp.concatenate([counts[:, None], pattern], axis=1).astype(jnp.float32).reshape(-1)
    info = jnp.concatenate([squares, table, jnp.zeros((PIECE - table.size,), jnp.float32)])
    info = jnp.broadcast_to(info[None, None], (ROWS, 8, 2 * PIECE))
    info = lax.all_to_all(info, ("core", "z"), 0, 0)[:, 0]
    away = jnp.arange(8, dtype=jnp.int32)
    nearby = (z - away) % 8
    line_info = info[jnp.concatenate([core * 8 + nearby, (1 - core) * 8 + nearby])]
    row_sq = line_info[:, :PIECE].reshape(ROWS, 1, PIECE)
    squares, rows[4], rows[5] = lax.optimization_barrier((squares, rows[4], rows[5]))
    col_sq = gather_pieces(jnp.broadcast_to(squares[None], (8, PIECE)))[:, 0]
    col_sq = col_sq.reshape(BLOCKS, WIDTH, 1)
    tables = line_info[:, PIECE:PIECE + table.size].reshape(ROWS, 2, slots + 1)
    mine = lax.dynamic_index_in_dim(tables.astype(jnp.int32), y // 2, 1, keepdims=False)

    j = jnp.arange(BLOCKS, dtype=jnp.int32)
    col_block = (z * 4 + (j // 2) * 2 + core) * 2 + j % 2
    hit = (mine[None, :, 1:] == col_block[:, None, None]) & (
        jnp.arange(slots, dtype=jnp.int32)[None, None, :] < mine[None, :, :1]
    )
    live = jnp.any(hit, axis=2)
    flat = live.reshape(TILES).astype(jnp.int32)
    order = jnp.arange(TILES, dtype=jnp.int32)
    before = jnp.sum(jnp.where(order[None, :] < order[:, None], flat[None, :], 0), axis=1)
    counted = jnp.sum(live.astype(jnp.int32), axis=1)
    even = counted + counted % 2
    block_start = jnp.sum(jnp.where(j[None, :] < j[:, None], even[None, :], 0), axis=1)
    block_before = jnp.sum(jnp.where(j[None, :] < j[:, None], counted[None, :], 0), axis=1)
    position = before + jnp.repeat(block_start - block_before, ROWS)
    spot = jnp.arange(TILES + 8, dtype=jnp.int32)
    pairs = jnp.max(
        jnp.where((position[None, :] <= spot[:, None]) & (flat[None, :] > 0), order[None, :], 0),
        axis=1,
    ).astype(jnp.int32)
    starts = (jnp.concatenate([block_start, jnp.sum(even)[None]]) // 2).astype(jnp.int32)
    own_tile = (xl * 2 + y // 2) * ROWS
    own_offset = ((y % 2) * 2 + xh) * PIECE
    meta = jnp.stack([jnp.sum(flat), own_offset, own_tile, z, y, xh * 2 + xl]).astype(jnp.int32)

    weights, keep, send, degree_keep, degree_send = build_weights(
        pairs, meta, starts, rows, cols, row_sq, col_sq
    )
    degree_sum = degree_keep + swap_cores(degree_send)
    high = lax.reduce_precision(degree_sum, 8, 7)
    low = degree_sum - high
    degree_rows = jnp.stack([high, low], axis=1).astype(jnp.bfloat16)
    degree_rows = jnp.concatenate([degree_rows, jnp.zeros((8, 14, PIECE), jnp.bfloat16)], axis=1)

    for iteration in range(ITERS):
        if iteration > 0:
            keep, send = spread_rows(pairs, meta, starts, weights, gathered)
        part = (keep + swap_cores(send).astype(jnp.float32)).astype(jnp.bfloat16)
        if iteration == 0:
            part = jnp.concatenate([part, degree_rows], axis=1)
        parts = lax.all_to_all(part, "z", 0, 0)
        summed = jnp.sum(parts.astype(jnp.float32), axis=0)
        if iteration == 0:
            degree_own = summed[tasks] + summed[tasks + 1]
            summed = summed[:tasks]
        labels = (PROPAGATE * summed / degree_own[None, :] + ANCHOR * seeded).astype(jnp.bfloat16)
        if iteration < ITERS - 1:
            gathered = gather_shifted(labels)
    return labels.T


def solution(mesh):
    split = Mesh(mesh.devices.reshape(SIZES), AXES)
    whole = ("z", "xl", "core", "y", "xh")
    blocks = ("z", "xl", "core")
    placed = (P(whole, None), P(whole, None), P(whole), P(blocks, None), P(blocks))
    return jax.shard_map(
        body, mesh=split, in_specs=placed, out_specs=P(whole, None), check_vma=False
    )
```

```python
import jax
import jax.numpy as jnp
from jax import lax
from jax.experimental import pallas as pl
from jax.experimental.pallas import tpu as pltpu
from jax.sharding import Mesh, PartitionSpec as P

ITERS = 3

WEIGHT_ROW = 0.6
WEIGHT_COL = 0.3
WEIGHT_SHARED = 0.1
SHARPNESS = 80.0
EPSILON = 1e-05
PROPAGATE = 0.8
ANCHOR = 0.2

AXES = ("y", "xh", "z", "xl", "core")
SIZES = (4, 2, 8, 2, 2)
PLANE = ("xl", "y", "xh")
PIECE = 128
EXTRA = 16
ROWS = 16
BLOCKS = 4
WIDTH = 512
TILES = ROWS * BLOCKS
VMEM_LIMIT = 48 * 1024 * 1024


def prepare_kernel(prints, activity, mask, extended, seeded):
    value = activity[...].astype(jnp.float32).T * mask[...].astype(jnp.float32)
    seeded[...] = value
    labels = value.astype(jnp.bfloat16)
    extended[:PIECE, :] = prints[...]
    for group in range(labels.shape[0] // EXTRA):
        extended[PIECE:, group * PIECE:(group + 1) * PIECE] = labels[
            group * EXTRA:(group + 1) * EXTRA, :
        ]


def prepare(prints, activity, mask):
    vmem = pl.BlockSpec(memory_space=pltpu.VMEM)
    return pl.pallas_call(
        prepare_kernel,
        out_shape=(
            jax.ShapeDtypeStruct((PIECE + EXTRA, prints.shape[1]), jnp.bfloat16),
            jax.ShapeDtypeStruct((activity.shape[1], PIECE), jnp.float32),
        ),
        in_specs=[vmem] * 3,
        out_specs=(vmem, vmem),
        name="prepare",
    )(prints, activity, mask[None])


def split_rows(z, total, keep, send):
    half = ROWS // 2
    for piece in range(half):
        place = lax.rem(z - piece + half, half)
        keep[piece] = total[place]
        send[piece] = total[half + place].astype(jnp.bfloat16)


def weights_kernel(pairs, meta, starts, *refs):
    rows = refs[:ROWS]
    (cols, row_sq, col_sq, weights, keep, send, degree_keep, degree_send,
     col_buf, row_buf, tile_buf, label_raw, labels, total, degree, inner_even, inner_odd,
     col_sem, row_sem, tile_sem, label_sem) = refs[ROWS:]
    live = starts[BLOCKS]
    own_offset = meta[1]
    own_tile = meta[2]
    z = meta[3]

    def row_copy(q, side, source):
        slot = lax.rem(q, 3)
        return pltpu.make_async_copy(
            rows[source], row_buf.at[slot, pl.ds(side * PIECE, PIECE)], row_sem.at[slot, side]
        )

    def start_rows(q):
        for side in range(2):
            wanted = lax.rem(pairs[2 * q + side], ROWS)
            for source in range(ROWS):
                @pl.when(wanted == source)
                def _():
                    row_copy(q, side, source).start()

    def col_copy(j):
        return pltpu.make_async_copy(
            cols.at[j % 2, :, j // 2, pl.ds(0, PIECE)], col_buf.at[j], col_sem.at[j]
        )

    def tile_copy(tile_id):
        return pltpu.make_async_copy(
            tile_buf.at[tile_id], weights.at[tile_id], tile_sem.at[tile_id]
        )

    col_copy(0).start()
    for first in range(2):
        @pl.when(first < live)
        def _():
            start_rows(first)
    label_copy = pltpu.make_async_copy(
        cols.at[:, :, :, pl.ds(PIECE, EXTRA)], label_raw, label_sem
    )
    label_copy.start()
    for j in range(1, BLOCKS):
        col_copy(j).start()
    degree[...] = jnp.zeros_like(degree)
    total[...] = jnp.zeros_like(total)
    label_copy.wait()
    for j in range(BLOCKS):
        for sub in range(WIDTH // PIECE):
            for group in range(labels.shape[1] // EXTRA):
                labels[
                    j, group * EXTRA:(group + 1) * EXTRA, sub * PIECE:(sub + 1) * PIECE
                ] = label_raw[j % 2, sub, j // 2, :, group * PIECE:(group + 1) * PIECE]
    lane = lax.broadcasted_iota(jnp.int32, (WIDTH, 2 * PIECE), 1)
    gap = jnp.where(
        lane < PIECE, lax.broadcasted_iota(jnp.int32, (WIDTH, 2 * PIECE), 0) - lane, -WIDTH
    )
    depth = col_buf.shape[-1]

    def arrive(q):
        j = pairs[2 * q] // ROWS

        @pl.when(q == starts[j])
        def _():
            pltpu.make_async_copy(
                cols.at[0, :, 0, pl.ds(0, PIECE)], col_buf.at[j], col_sem.at[j]
            ).wait()

        row_copy(q, 0, 0).wait()
        row_copy(q, 1, 0).wait()

    def multiply(q):
        return lax.dot_general(
            col_buf[pairs[2 * q] // ROWS].reshape(WIDTH, depth), row_buf[lax.rem(q, 3)],
            (((1,), (1,)), ((), ())),
            preferred_element_type=jnp.float32,
        )

    @pl.when(live > 0)
    def _():
        arrive(0)
        inner_even[...] = multiply(0)

    def step(q, current, following):
        @pl.when(q + 2 < live)
        def _():
            start_rows(q + 2)

        @pl.when(q + 1 < live)
        def _():
            arrive(q + 1)

        following[...] = multiply(jnp.minimum(q + 1, live - 1))
        one = pairs[2 * q]
        two = pairs[2 * q + 1]
        j = one // ROWS
        place_one = lax.rem(one, ROWS)
        place_two = lax.rem(two, ROWS)
        inner = current[...]
        row_part = jnp.concatenate([row_sq[place_one], row_sq[place_two]], axis=1)
        ratio = inner / (
            WEIGHT_ROW * row_part
            + WEIGHT_COL * col_sq[j]
            + WEIGHT_SHARED * inner
            + EPSILON
        )
        offset = jnp.where(one == own_tile, own_offset, -2 * WIDTH)
        value = jnp.where(gap == offset, 0.0, jnp.exp(SHARPNESS * (ratio - 0.5)))
        half = value.astype(jnp.bfloat16)
        spread = jnp.dot(labels[j], half, preferred_element_type=jnp.float32)
        sums = jnp.sum(value, axis=0, keepdims=True)
        tile_buf[one] = half[:, :PIECE]
        tile_copy(one).start()
        total[place_one] += spread[:, :PIECE]
        degree[pl.ds(place_one, 1), :] += sums[:, :PIECE]

        @pl.when(one != two)
        def _():
            tile_buf[two] = half[:, PIECE:]
            tile_copy(two).start()
            total[place_two] += spread[:, PIECE:]
            degree[pl.ds(place_two, 1), :] += sums[:, PIECE:]

    def steps(i, carry):
        step(2 * i, inner_even, inner_odd)

        @pl.when(2 * i + 1 < live)
        def _():
            step(2 * i + 1, inner_odd, inner_even)

        return carry

    lax.fori_loop(0, (live + 1) // 2, steps, 0)
    for j in range(BLOCKS):
        @pl.when(starts[j] == starts[j + 1])
        def _():
            pltpu.make_async_copy(
                cols.at[0, :, 0, pl.ds(0, PIECE)], col_buf.at[j], col_sem.at[j]
            ).wait()

    split_rows(z, total, keep, send)
    half_rows = ROWS // 2
    for piece in range(half_rows):
        place = lax.rem(z - piece + half_rows, half_rows)
        degree_keep[piece:piece + 1, :] = degree[pl.ds(place, 1), :]
        degree_send[piece:piece + 1, :] = degree[pl.ds(half_rows + place, 1), :]

    def finish(q, carry):
        tile_copy(pairs[2 * q]).wait()

        @pl.when(pairs[2 * q] != pairs[2 * q + 1])
        def _():
            tile_copy(pairs[2 * q + 1]).wait()

        return carry

    lax.fori_loop(0, live, finish, 0)


def build_weights(pairs, meta, starts, rows, cols, row_sq, col_sq):
    smem = pl.BlockSpec(memory_space=pltpu.SMEM)
    vmem = pl.BlockSpec(memory_space=pltpu.VMEM)
    hbm = pl.BlockSpec(memory_space=pl.ANY)
    depth = cols.shape[-1]
    tasks = depth * EXTRA // PIECE
    return pl.pallas_call(
        weights_kernel,
        out_shape=(
            jax.ShapeDtypeStruct((TILES, WIDTH, PIECE), jnp.bfloat16),
            jax.ShapeDtypeStruct((ROWS // 2, tasks, PIECE), jnp.float32),
            jax.ShapeDtypeStruct((ROWS // 2, tasks, PIECE), jnp.bfloat16),
            jax.ShapeDtypeStruct((ROWS // 2, PIECE), jnp.float32),
            jax.ShapeDtypeStruct((ROWS // 2, PIECE), jnp.float32),
        ),
        in_specs=[smem, smem, smem] + [hbm] * ROWS + [hbm, vmem, vmem],
        out_specs=(hbm, vmem, vmem, vmem, vmem),
        scratch_shapes=[
            pltpu.VMEM((BLOCKS, WIDTH // PIECE, PIECE, depth), jnp.bfloat16),
            pltpu.VMEM((3, 2 * PIECE, depth), jnp.bfloat16),
            pltpu.VMEM((TILES, WIDTH, PIECE), jnp.bfloat16),
            pltpu.VMEM((2, 4, 2, EXTRA, depth), jnp.bfloat16),
            pltpu.VMEM((BLOCKS, tasks, WIDTH), jnp.bfloat16),
            pltpu.VMEM((ROWS, tasks, PIECE), jnp.float32),
            pltpu.VMEM((ROWS, PIECE), jnp.float32),
            pltpu.VMEM((WIDTH, 2 * PIECE), jnp.float32),
            pltpu.VMEM((WIDTH, 2 * PIECE), jnp.float32),
            pltpu.SemaphoreType.DMA((BLOCKS,)),
            pltpu.SemaphoreType.DMA((3, 2)),
            pltpu.SemaphoreType.DMA((TILES,)),
            pltpu.SemaphoreType.DMA,
        ],
        compiler_params=pltpu.CompilerParams(vmem_limit_bytes=VMEM_LIMIT),
        cost_estimate=pl.CostEstimate(
            flops=16 * 2 * PIECE * WIDTH * depth,
            bytes_accessed=2 * (ROWS + 16) * PIECE * depth,
            transcendentals=16 * PIECE * WIDTH,
        ),
        name="weights",
    )(pairs, meta, starts, *rows, cols, row_sq, col_sq)


def spread_kernel(pairs, meta, starts, weights, pieces, keep, send, total, tile_buf, tile_sem):
    live = starts[BLOCKS]
    z = meta[3]
    half = ROWS // 2

    def tile_copy(q, side):
        return pltpu.make_async_copy(
            weights.at[pairs[2 * q + side]],
            tile_buf.at[q, :, pl.ds(side * PIECE, PIECE)],
            tile_sem.at[q, side],
        )

    def begin(q, carry):
        tile_copy(q, 0).start()

        @pl.when(pairs[2 * q] != pairs[2 * q + 1])
        def _():
            tile_copy(q, 1).start()

        return carry

    lax.fori_loop(0, live, begin, 0)
    total[...] = jnp.zeros_like(total)

    def add(tile_id, value):
        a = lax.rem(tile_id, ROWS)
        side = a // half
        place = side * half + lax.rem(z - lax.rem(a, half) + half, half)
        total[place] += value

    def pair(q, carry):
        one = pairs[2 * q]
        two = pairs[2 * q + 1]
        tile_copy(q, 0).wait()

        @pl.when(one != two)
        def _():
            tile_copy(q, 1).wait()

        j = one // ROWS
        spread = jnp.dot(
            jnp.concatenate([pieces[j * 4 + sub] for sub in range(WIDTH // PIECE)], axis=1),
            tile_buf[q], preferred_element_type=jnp.float32,
        )
        add(one, spread[:, :PIECE])

        @pl.when(one != two)
        def _():
            add(two, spread[:, PIECE:])

        return carry

    lax.fori_loop(0, live, pair, 0)
    keep[...] = total[:half]
    send[...] = total[half:].astype(jnp.bfloat16)


def spread_rows(pairs, meta, starts, weights, pieces):
    smem = pl.BlockSpec(memory_space=pltpu.SMEM)
    vmem = pl.BlockSpec(memory_space=pltpu.VMEM)
    hbm = pl.BlockSpec(memory_space=pl.ANY)
    tasks = pieces.shape[1]
    return pl.pallas_call(
        spread_kernel,
        out_shape=(
            jax.ShapeDtypeStruct((ROWS // 2, tasks, PIECE), jnp.float32),
            jax.ShapeDtypeStruct((ROWS // 2, tasks, PIECE), jnp.bfloat16),
        ),
        in_specs=[smem, smem, smem, hbm, vmem],
        out_specs=(vmem, vmem),
        scratch_shapes=[
            pltpu.VMEM((ROWS, tasks, PIECE), jnp.float32),
            pltpu.VMEM((TILES // 2, WIDTH, 2 * PIECE), jnp.bfloat16),
            pltpu.SemaphoreType.DMA((TILES // 2, 2)),
        ],
        compiler_params=pltpu.CompilerParams(vmem_limit_bytes=VMEM_LIMIT),
        name="spread",
    )(pairs, meta, starts, weights, pieces)


def swap_cores(value):
    return lax.ppermute(value, "core", [(0, 1), (1, 0)])


def gather_pieces(piece):
    copies = jnp.broadcast_to(piece[None], (ROWS,) + piece.shape)
    return lax.all_to_all(copies, PLANE, 0, 0)


def body(fingerprints, activity, label_mask, pattern, counts):
    y, xh, z, xl, core = [lax.axis_index(axis) for axis in AXES]
    depth = fingerprints.shape[1]
    slots = pattern.shape[1]
    tasks = activity.shape[1]
    extended, seeded = prepare(fingerprints, activity, label_mask)
    cols = lax.all_gather(extended, ("y", "xh", "xl"), axis=0, tiled=True)
    cols = cols.reshape(2, 4, 2, PIECE + EXTRA, depth)

    upward = [fingerprints]
    for step in range(4):
        upward.append(lax.ppermute(upward[-1], "z", [(i, (i + 1) % 8) for i in range(8)]))
    downward = [fingerprints]
    for step in range(3):
        downward.append(lax.ppermute(downward[-1], "z", [(i, (i + 7) % 8) for i in range(8)]))
    rows = upward + [downward[3], downward[2], downward[1]]
    rows = rows + [swap_cores(row) for row in rows]

    squares = jnp.sum(jnp.square(fingerprints.astype(jnp.float32)), axis=1)
    table = jnp.concatenate([counts[:, None], pattern], axis=1).astype(jnp.float32).reshape(-1)
    info = jnp.concatenate([squares, table, jnp.zeros((PIECE - table.size,), jnp.float32)])
    info = jnp.broadcast_to(info[None, None], (ROWS, 8, 2 * PIECE))
    info = lax.all_to_all(info, ("core", "z"), 0, 0)[:, 0]
    away = jnp.arange(8, dtype=jnp.int32)
    nearby = (z - away) % 8
    line_info = info[jnp.concatenate([core * 8 + nearby, (1 - core) * 8 + nearby])]
    row_sq = line_info[:, :PIECE].reshape(ROWS, 1, PIECE)
    squares, rows[4], rows[5] = lax.optimization_barrier((squares, rows[4], rows[5]))
    col_sq = gather_pieces(jnp.broadcast_to(squares[None], (8, PIECE)))[:, 0]
    col_sq = col_sq.reshape(BLOCKS, WIDTH, 1)
    tables = line_info[:, PIECE:PIECE + table.size].reshape(ROWS, 2, slots + 1)
    mine = lax.dynamic_index_in_dim(tables.astype(jnp.int32), y // 2, 1, keepdims=False)

    j = jnp.arange(BLOCKS, dtype=jnp.int32)
    col_block = (z * 4 + (j // 2) * 2 + core) * 2 + j % 2
    hit = (mine[None, :, 1:] == col_block[:, None, None]) & (
        jnp.arange(slots, dtype=jnp.int32)[None, None, :] < mine[None, :, :1]
    )
    live = jnp.any(hit, axis=2)
    flat = live.reshape(TILES).astype(jnp.int32)
    order = jnp.arange(TILES, dtype=jnp.int32)
    before = jnp.sum(jnp.where(order[None, :] < order[:, None], flat[None, :], 0), axis=1)
    counted = jnp.sum(live.astype(jnp.int32), axis=1)
    even = counted + counted % 2
    block_start = jnp.sum(jnp.where(j[None, :] < j[:, None], even[None, :], 0), axis=1)
    block_before = jnp.sum(jnp.where(j[None, :] < j[:, None], counted[None, :], 0), axis=1)
    position = before + jnp.repeat(block_start - block_before, ROWS)
    spot = jnp.arange(TILES + 8, dtype=jnp.int32)
    pairs = jnp.max(
        jnp.where((position[None, :] <= spot[:, None]) & (flat[None, :] > 0), order[None, :], 0),
        axis=1,
    ).astype(jnp.int32)
    starts = (jnp.concatenate([block_start, jnp.sum(even)[None]]) // 2).astype(jnp.int32)
    own_tile = (xl * 2 + y // 2) * ROWS
    own_offset = ((y % 2) * 2 + xh) * PIECE
    meta = jnp.stack([jnp.sum(flat), own_offset, own_tile, z]).astype(jnp.int32)

    weights, keep, send, degree_keep, degree_send = build_weights(
        pairs, meta, starts, rows, cols, row_sq, col_sq
    )
    degree_sum = degree_keep + swap_cores(degree_send)
    high = lax.reduce_precision(degree_sum, 8, 7)
    low = degree_sum - high
    degree_rows = jnp.stack([high, low], axis=1).astype(jnp.bfloat16)
    degree_rows = jnp.concatenate([degree_rows, jnp.zeros((8, 14, PIECE), jnp.bfloat16)], axis=1)

    for iteration in range(ITERS):
        if iteration > 0:
            keep, send = spread_rows(pairs, meta, starts, weights, gathered)
        part = (keep + swap_cores(send).astype(jnp.float32)).astype(jnp.bfloat16)
        if iteration == 0:
            part = jnp.concatenate([part, degree_rows], axis=1)
        parts = lax.all_to_all(part, "z", 0, 0)
        summed = jnp.sum(parts.astype(jnp.float32), axis=0)
        if iteration == 0:
            degree_own = summed[tasks] + summed[tasks + 1]
            summed = summed[:tasks]
        labels = (PROPAGATE * summed / degree_own[None, :] + ANCHOR * seeded).astype(jnp.bfloat16)
        if iteration < ITERS - 1:
            gathered = gather_pieces(labels)
    return labels.T


def solution(mesh):
    split = Mesh(mesh.devices.reshape(SIZES), AXES)
    whole = ("z", "xl", "core", "y", "xh")
    blocks = ("z", "xl", "core")
    placed = (P(whole, None), P(whole, None), P(whole), P(blocks, None), P(blocks))
    return jax.shard_map(
        body, mesh=split, in_specs=placed, out_specs=P(whole, None), check_vma=False
    )
```

```python
import jax
import jax.numpy as jnp
from jax import lax
from jax.experimental import pallas as pl
from jax.experimental.pallas import tpu as pltpu
from jax.sharding import Mesh, PartitionSpec as P

ITERS = 3

WEIGHT_ROW = 0.6
WEIGHT_COL = 0.3
WEIGHT_SHARED = 0.1
SHARPNESS = 80.0
EPSILON = 1e-05
PROPAGATE = 0.8
ANCHOR = 0.2

AXES = ("y", "xh", "z", "xl", "core")
SIZES = (4, 2, 8, 2, 2)
PLANE = ("xl", "y", "xh")
PIECE = 128
EXTRA = 16
ROWS = 16
BLOCKS = 4
WIDTH = 512
TILES = ROWS * BLOCKS
VMEM_LIMIT = 48 * 1024 * 1024


def prepare_kernel(prints, activity, mask, extended, seeded):
    value = activity[...].astype(jnp.float32).T * mask[...].astype(jnp.float32)
    seeded[...] = value
    labels = value.astype(jnp.bfloat16)
    extended[:PIECE, :] = prints[...]
    for group in range(labels.shape[0] // EXTRA):
        extended[PIECE:, group * PIECE:(group + 1) * PIECE] = labels[
            group * EXTRA:(group + 1) * EXTRA, :
        ]


def prepare(prints, activity, mask):
    vmem = pl.BlockSpec(memory_space=pltpu.VMEM)
    return pl.pallas_call(
        prepare_kernel,
        out_shape=(
            jax.ShapeDtypeStruct((PIECE + EXTRA, prints.shape[1]), jnp.bfloat16),
            jax.ShapeDtypeStruct((activity.shape[1], PIECE), jnp.float32),
        ),
        in_specs=[vmem] * 3,
        out_specs=(vmem, vmem),
        name="prepare",
    )(prints, activity, mask[None])


def split_rows(z, total, keep, send):
    half = ROWS // 2
    for piece in range(half):
        place = lax.rem(z - piece + half, half)
        keep[piece] = total[place]
        send[piece] = total[half + place].astype(jnp.bfloat16)


def weights_kernel(pairs, meta, starts, *refs):
    rows = refs[:ROWS]
    (cols, row_sq, col_sq, weights, keep, send,
     col_buf, row_buf, tile_buf, label_raw, labels, total, degree, inner_even, inner_odd,
     col_sem, row_sem, tile_sem, label_sem) = refs[ROWS:]
    live = starts[BLOCKS]
    own_offset = meta[1]
    own_tile = meta[2]
    z = meta[3]

    def row_copy(q, side, source):
        slot = lax.rem(q, 3)
        return pltpu.make_async_copy(
            rows[source], row_buf.at[slot, pl.ds(side * PIECE, PIECE)], row_sem.at[slot, side]
        )

    def start_rows(q):
        for side in range(2):
            wanted = lax.rem(pairs[2 * q + side], ROWS)
            for source in range(ROWS):
                @pl.when(wanted == source)
                def _():
                    row_copy(q, side, source).start()

    def col_copy(j):
        return pltpu.make_async_copy(
            cols.at[j % 2, :, j // 2, pl.ds(0, PIECE)], col_buf.at[j], col_sem.at[j]
        )

    def tile_copy(tile_id):
        return pltpu.make_async_copy(
            tile_buf.at[tile_id], weights.at[tile_id], tile_sem.at[tile_id]
        )

    col_copy(0).start()
    for first in range(2):
        @pl.when(first < live)
        def _():
            start_rows(first)
    label_copy = pltpu.make_async_copy(
        cols.at[:, :, :, pl.ds(PIECE, EXTRA)], label_raw, label_sem
    )
    label_copy.start()
    for j in range(1, BLOCKS):
        col_copy(j).start()
    degree[...] = jnp.zeros_like(degree)
    total[...] = jnp.zeros_like(total)
    label_copy.wait()
    for j in range(BLOCKS):
        for sub in range(WIDTH // PIECE):
            for group in range(labels.shape[1] // EXTRA):
                labels[
                    j, group * EXTRA:(group + 1) * EXTRA, sub * PIECE:(sub + 1) * PIECE
                ] = label_raw[j % 2, sub, j // 2, :, group * PIECE:(group + 1) * PIECE]
    lane = lax.broadcasted_iota(jnp.int32, (WIDTH, 2 * PIECE), 1)
    gap = jnp.where(
        lane < PIECE, lax.broadcasted_iota(jnp.int32, (WIDTH, 2 * PIECE), 0) - lane, -WIDTH
    )
    depth = col_buf.shape[-1]

    def arrive(q):
        j = pairs[2 * q] // ROWS

        @pl.when(q == starts[j])
        def _():
            pltpu.make_async_copy(
                cols.at[0, :, 0, pl.ds(0, PIECE)], col_buf.at[j], col_sem.at[j]
            ).wait()

        row_copy(q, 0, 0).wait()
        row_copy(q, 1, 0).wait()

    def multiply(q):
        return lax.dot_general(
            col_buf[pairs[2 * q] // ROWS].reshape(WIDTH, depth), row_buf[lax.rem(q, 3)],
            (((1,), (1,)), ((), ())),
            preferred_element_type=jnp.float32,
        )

    @pl.when(live > 0)
    def _():
        arrive(0)
        inner_even[...] = multiply(0)

    def step(q, current, following):
        @pl.when(q + 2 < live)
        def _():
            start_rows(q + 2)

        @pl.when(q + 1 < live)
        def _():
            arrive(q + 1)

        following[...] = multiply(jnp.minimum(q + 1, live - 1))
        one = pairs[2 * q]
        two = pairs[2 * q + 1]
        j = one // ROWS
        place_one = lax.rem(one, ROWS)
        place_two = lax.rem(two, ROWS)
        inner = current[...]
        row_part = jnp.concatenate([row_sq[place_one], row_sq[place_two]], axis=1)
        ratio = inner / (
            WEIGHT_ROW * row_part
            + WEIGHT_COL * col_sq[j]
            + WEIGHT_SHARED * inner
            + EPSILON
        )
        offset = jnp.where(one == own_tile, own_offset, -2 * WIDTH)
        value = jnp.where(gap == offset, 0.0, jnp.exp(SHARPNESS * (ratio - 0.5)))
        half = value.astype(jnp.bfloat16)
        spread = jnp.dot(labels[j], half, preferred_element_type=jnp.float32)
        sums = jnp.sum(value, axis=0, keepdims=True)
        tile_buf[one] = half[:, :PIECE]
        tile_copy(one).start()
        total[place_one] += spread[:, :PIECE]
        degree[pl.ds(place_one, 1), :] += sums[:, :PIECE]

        @pl.when(one != two)
        def _():
            tile_buf[two] = half[:, PIECE:]
            tile_copy(two).start()
            total[place_two] += spread[:, PIECE:]
            degree[pl.ds(place_two, 1), :] += sums[:, PIECE:]

    def steps(i, carry):
        step(2 * i, inner_even, inner_odd)

        @pl.when(2 * i + 1 < live)
        def _():
            step(2 * i + 1, inner_odd, inner_even)

        return carry

    lax.fori_loop(0, (live + 1) // 2, steps, 0)
    for j in range(BLOCKS):
        @pl.when(starts[j] == starts[j + 1])
        def _():
            pltpu.make_async_copy(
                cols.at[0, :, 0, pl.ds(0, PIECE)], col_buf.at[j], col_sem.at[j]
            ).wait()

    half_rows = ROWS // 2
    tasks = labels.shape[1]
    line = lax.broadcasted_iota(jnp.int32, (EXTRA, PIECE), 0)

    def degree_lines(where, first):
        whole = degree[pl.ds(where, 1), :]
        high = whole.astype(jnp.bfloat16).astype(jnp.float32)
        return jnp.where(
            line == first, high, jnp.where(line == first + 1, whole - high, 0.0)
        )

    for piece in range(half_rows):
        place = lax.rem(z - piece + half_rows, half_rows)
        keep[piece, :tasks, :] = total[place]
        keep[piece, tasks:, :] = degree_lines(place, 0)
        send[piece, :tasks, :] = total[half_rows + place].astype(jnp.bfloat16)
        send[piece, tasks:, :] = degree_lines(half_rows + place, 2).astype(jnp.bfloat16)

    def finish(q, carry):
        tile_copy(pairs[2 * q]).wait()

        @pl.when(pairs[2 * q] != pairs[2 * q + 1])
        def _():
            tile_copy(pairs[2 * q + 1]).wait()

        return carry

    lax.fori_loop(0, live, finish, 0)


def build_weights(pairs, meta, starts, rows, cols, row_sq, col_sq):
    smem = pl.BlockSpec(memory_space=pltpu.SMEM)
    vmem = pl.BlockSpec(memory_space=pltpu.VMEM)
    hbm = pl.BlockSpec(memory_space=pl.ANY)
    depth = cols.shape[-1]
    tasks = depth * EXTRA // PIECE
    return pl.pallas_call(
        weights_kernel,
        out_shape=(
            jax.ShapeDtypeStruct((TILES, WIDTH, PIECE), jnp.bfloat16),
            jax.ShapeDtypeStruct((ROWS // 2, tasks + EXTRA, PIECE), jnp.float32),
            jax.ShapeDtypeStruct((ROWS // 2, tasks + EXTRA, PIECE), jnp.bfloat16),
        ),
        in_specs=[smem, smem, smem] + [hbm] * ROWS + [hbm, vmem, vmem],
        out_specs=(hbm, vmem, vmem),
        scratch_shapes=[
            pltpu.VMEM((BLOCKS, WIDTH // PIECE, PIECE, depth), jnp.bfloat16),
            pltpu.VMEM((3, 2 * PIECE, depth), jnp.bfloat16),
            pltpu.VMEM((TILES, WIDTH, PIECE), jnp.bfloat16),
            pltpu.VMEM((2, 4, 2, EXTRA, depth), jnp.bfloat16),
            pltpu.VMEM((BLOCKS, tasks, WIDTH), jnp.bfloat16),
            pltpu.VMEM((ROWS, tasks, PIECE), jnp.float32),
            pltpu.VMEM((ROWS, PIECE), jnp.float32),
            pltpu.VMEM((WIDTH, 2 * PIECE), jnp.float32),
            pltpu.VMEM((WIDTH, 2 * PIECE), jnp.float32),
            pltpu.SemaphoreType.DMA((BLOCKS,)),
            pltpu.SemaphoreType.DMA((3, 2)),
            pltpu.SemaphoreType.DMA((TILES,)),
            pltpu.SemaphoreType.DMA,
        ],
        compiler_params=pltpu.CompilerParams(vmem_limit_bytes=VMEM_LIMIT),
        cost_estimate=pl.CostEstimate(
            flops=16 * 2 * PIECE * WIDTH * depth,
            bytes_accessed=2 * (ROWS + 16) * PIECE * depth,
            transcendentals=16 * PIECE * WIDTH,
        ),
        name="weights",
    )(pairs, meta, starts, *rows, cols, row_sq, col_sq)


def spread_kernel(pairs, meta, starts, weights, pieces, keep, send, total, tile_buf, tile_sem):
    live = starts[BLOCKS]
    z = meta[3]
    half = ROWS // 2

    def tile_copy(q, side):
        return pltpu.make_async_copy(
            weights.at[pairs[2 * q + side]],
            tile_buf.at[q, :, pl.ds(side * PIECE, PIECE)],
            tile_sem.at[q, side],
        )

    def begin(q, carry):
        tile_copy(q, 0).start()

        @pl.when(pairs[2 * q] != pairs[2 * q + 1])
        def _():
            tile_copy(q, 1).start()

        return carry

    lax.fori_loop(0, live, begin, 0)
    total[...] = jnp.zeros_like(total)

    def add(tile_id, value):
        a = lax.rem(tile_id, ROWS)
        side = a // half
        place = side * half + lax.rem(z - lax.rem(a, half) + half, half)
        total[place] += value

    def pair(q, carry):
        one = pairs[2 * q]
        two = pairs[2 * q + 1]
        tile_copy(q, 0).wait()

        @pl.when(one != two)
        def _():
            tile_copy(q, 1).wait()

        j = one // ROWS
        spread = jnp.dot(
            jnp.concatenate([pieces[j * 4 + sub] for sub in range(WIDTH // PIECE)], axis=1),
            tile_buf[q], preferred_element_type=jnp.float32,
        )
        add(one, spread[:, :PIECE])

        @pl.when(one != two)
        def _():
            add(two, spread[:, PIECE:])

        return carry

    lax.fori_loop(0, live, pair, 0)
    keep[...] = total[:half]
    send[...] = total[half:].astype(jnp.bfloat16)


def spread_rows(pairs, meta, starts, weights, pieces):
    smem = pl.BlockSpec(memory_space=pltpu.SMEM)
    vmem = pl.BlockSpec(memory_space=pltpu.VMEM)
    hbm = pl.BlockSpec(memory_space=pl.ANY)
    tasks = pieces.shape[1]
    return pl.pallas_call(
        spread_kernel,
        out_shape=(
            jax.ShapeDtypeStruct((ROWS // 2, tasks, PIECE), jnp.float32),
            jax.ShapeDtypeStruct((ROWS // 2, tasks, PIECE), jnp.bfloat16),
        ),
        in_specs=[smem, smem, smem, hbm, vmem],
        out_specs=(vmem, vmem),
        scratch_shapes=[
            pltpu.VMEM((ROWS, tasks, PIECE), jnp.float32),
            pltpu.VMEM((TILES // 2, WIDTH, 2 * PIECE), jnp.bfloat16),
            pltpu.SemaphoreType.DMA((TILES // 2, 2)),
        ],
        compiler_params=pltpu.CompilerParams(vmem_limit_bytes=VMEM_LIMIT),
        name="spread",
    )(pairs, meta, starts, weights, pieces)


def swap_cores(value):
    return lax.ppermute(value, "core", [(0, 1), (1, 0)])


def gather_pieces(piece):
    copies = jnp.broadcast_to(piece[None], (ROWS,) + piece.shape)
    return lax.all_to_all(copies, PLANE, 0, 0)


def body(fingerprints, activity, label_mask, pattern, counts):
    y, xh, z, xl, core = [lax.axis_index(axis) for axis in AXES]
    depth = fingerprints.shape[1]
    slots = pattern.shape[1]
    tasks = activity.shape[1]
    extended, seeded = prepare(fingerprints, activity, label_mask)
    cols = lax.all_gather(extended, ("y", "xh", "xl"), axis=0, tiled=True)
    cols = cols.reshape(2, 4, 2, PIECE + EXTRA, depth)

    upward = [fingerprints]
    for step in range(4):
        upward.append(lax.ppermute(upward[-1], "z", [(i, (i + 1) % 8) for i in range(8)]))
    downward = [fingerprints]
    for step in range(3):
        downward.append(lax.ppermute(downward[-1], "z", [(i, (i + 7) % 8) for i in range(8)]))
    rows = upward + [downward[3], downward[2], downward[1]]
    rows = rows + [swap_cores(row) for row in rows]

    squares = jnp.sum(jnp.square(fingerprints.astype(jnp.float32)), axis=1)
    table = jnp.concatenate([counts[:, None], pattern], axis=1).astype(jnp.float32).reshape(-1)
    info = jnp.concatenate([squares, table, jnp.zeros((PIECE - table.size,), jnp.float32)])
    info = jnp.broadcast_to(info[None, None], (ROWS, 8, 2 * PIECE))
    info = lax.all_to_all(info, ("core", "z"), 0, 0)[:, 0]
    away = jnp.arange(8, dtype=jnp.int32)
    nearby = (z - away) % 8
    line_info = info[jnp.concatenate([core * 8 + nearby, (1 - core) * 8 + nearby])]
    row_sq = line_info[:, :PIECE].reshape(ROWS, 1, PIECE)
    squares, rows[4], rows[5] = lax.optimization_barrier((squares, rows[4], rows[5]))
    col_sq = gather_pieces(jnp.broadcast_to(squares[None], (8, PIECE)))[:, 0]
    col_sq = col_sq.reshape(BLOCKS, WIDTH, 1)
    tables = line_info[:, PIECE:PIECE + table.size].reshape(ROWS, 2, slots + 1)
    mine = lax.dynamic_index_in_dim(tables.astype(jnp.int32), y // 2, 1, keepdims=False)

    j = jnp.arange(BLOCKS, dtype=jnp.int32)
    col_block = (z * 4 + (j // 2) * 2 + core) * 2 + j % 2
    hit = (mine[None, :, 1:] == col_block[:, None, None]) & (
        jnp.arange(slots, dtype=jnp.int32)[None, None, :] < mine[None, :, :1]
    )
    live = jnp.any(hit, axis=2)
    flat = live.reshape(TILES).astype(jnp.int32)
    order = jnp.arange(TILES, dtype=jnp.int32)
    before = jnp.sum(jnp.where(order[None, :] < order[:, None], flat[None, :], 0), axis=1)
    counted = jnp.sum(live.astype(jnp.int32), axis=1)
    even = counted + counted % 2
    block_start = jnp.sum(jnp.where(j[None, :] < j[:, None], even[None, :], 0), axis=1)
    block_before = jnp.sum(jnp.where(j[None, :] < j[:, None], counted[None, :], 0), axis=1)
    position = before + jnp.repeat(block_start - block_before, ROWS)
    spot = jnp.arange(TILES + 8, dtype=jnp.int32)
    pairs = jnp.max(
        jnp.where((position[None, :] <= spot[:, None]) & (flat[None, :] > 0), order[None, :], 0),
        axis=1,
    ).astype(jnp.int32)
    starts = (jnp.concatenate([block_start, jnp.sum(even)[None]]) // 2).astype(jnp.int32)
    own_tile = (xl * 2 + y // 2) * ROWS
    own_offset = ((y % 2) * 2 + xh) * PIECE
    meta = jnp.stack([jnp.sum(flat), own_offset, own_tile, z]).astype(jnp.int32)

    weights, keep, send = build_weights(
        pairs, meta, starts, rows, cols, row_sq, col_sq
    )

    for iteration in range(ITERS):
        if iteration > 0:
            keep, send = spread_rows(pairs, meta, starts, weights, gathered)
        part = (keep + swap_cores(send).astype(jnp.float32)).astype(jnp.bfloat16)
        parts = lax.all_to_all(part, "z", 0, 0)
        summed = jnp.sum(parts.astype(jnp.float32), axis=0)
        if iteration == 0:
            degree_own = jnp.sum(summed[tasks:tasks + 4], axis=0)
            summed = summed[:tasks]
        labels = (PROPAGATE * summed / degree_own[None, :] + ANCHOR * seeded).astype(jnp.bfloat16)
        if iteration < ITERS - 1:
            gathered = gather_pieces(labels)
    return labels.T


def solution(mesh):
    split = Mesh(mesh.devices.reshape(SIZES), AXES)
    whole = ("z", "xl", "core", "y", "xh")
    blocks = ("z", "xl", "core")
    placed = (P(whole, None), P(whole, None), P(whole), P(blocks, None), P(blocks))
    return jax.shard_map(
        body, mesh=split, in_specs=placed, out_specs=P(whole, None), check_vma=False
    )
```

```python
import jax
import jax.numpy as jnp
from jax import lax
from jax.experimental import pallas as pl
from jax.experimental.pallas import tpu as pltpu
from jax.sharding import Mesh, PartitionSpec as P

ITERS = 3

WEIGHT_ROW = 0.6
WEIGHT_COL = 0.3
WEIGHT_SHARED = 0.1
SHARPNESS = 80.0
EPSILON = 1e-05
PROPAGATE = 0.8
ANCHOR = 0.2

AXES = ("y", "xh", "z", "xl", "core")
SIZES = (4, 2, 8, 2, 2)
PLANE = ("xl", "y", "xh")
PIECE = 128
EXTRA = 16
ROWS = 16
BLOCKS = 4
WIDTH = 512
TILES = ROWS * BLOCKS
VMEM_LIMIT = 48 * 1024 * 1024


def prepare_kernel(prints, activity, mask, extended, seeded):
    value = activity[...].astype(jnp.float32).T * mask[...].astype(jnp.float32)
    seeded[...] = value
    labels = value.astype(jnp.bfloat16)
    extended[:PIECE, :] = prints[...]
    for group in range(labels.shape[0] // EXTRA):
        extended[PIECE:, group * PIECE:(group + 1) * PIECE] = labels[
            group * EXTRA:(group + 1) * EXTRA, :
        ]


def prepare(prints, activity, mask):
    vmem = pl.BlockSpec(memory_space=pltpu.VMEM)
    return pl.pallas_call(
        prepare_kernel,
        out_shape=(
            jax.ShapeDtypeStruct((PIECE + EXTRA, prints.shape[1]), jnp.bfloat16),
            jax.ShapeDtypeStruct((activity.shape[1], PIECE), jnp.float32),
        ),
        in_specs=[vmem] * 3,
        out_specs=(vmem, vmem),
        name="prepare",
    )(prints, activity, mask[None])


def split_rows(z, total, keep, send):
    half = ROWS // 2
    for piece in range(half):
        place = lax.rem(z - piece + half, half)
        keep[piece] = total[place]
        send[piece] = total[half + place].astype(jnp.bfloat16)


def weights_kernel(pairs, meta, starts, *refs):
    rows = refs[:ROWS]
    (cols, row_sq, col_sq, weights, keep, send, degree_keep, degree_send,
     col_buf, row_buf, tile_buf, label_raw, labels, total, degree, inner_even, inner_odd,
     col_sem, row_sem, tile_sem, label_sem) = refs[ROWS:]
    live = starts[BLOCKS]
    own_offset = meta[1]
    own_tile = meta[2]
    z = meta[3]

    def row_copy(q, side, source):
        slot = lax.rem(q, 3)
        return pltpu.make_async_copy(
            rows[source], row_buf.at[slot, pl.ds(side * PIECE, PIECE)], row_sem.at[slot, side]
        )

    def start_rows(q):
        for side in range(2):
            wanted = lax.rem(pairs[2 * q + side], ROWS)
            for source in range(ROWS):
                @pl.when(wanted == source)
                def _():
                    row_copy(q, side, source).start()

    def col_copy(j):
        return pltpu.make_async_copy(
            cols.at[j % 2, :, j // 2, pl.ds(0, PIECE)], col_buf.at[j], col_sem.at[j]
        )

    def tile_copy(tile_id):
        return pltpu.make_async_copy(
            tile_buf.at[tile_id], weights.at[tile_id], tile_sem.at[tile_id]
        )

    col_copy(0).start()
    for first in range(2):
        @pl.when(first < live)
        def _():
            start_rows(first)
    label_copy = pltpu.make_async_copy(
        cols.at[:, :, :, pl.ds(PIECE, EXTRA)], label_raw, label_sem
    )
    label_copy.start()
    for j in range(1, BLOCKS):
        col_copy(j).start()
    degree[...] = jnp.zeros_like(degree)
    total[...] = jnp.zeros_like(total)
    label_copy.wait()
    for j in range(BLOCKS):
        for sub in range(WIDTH // PIECE):
            for group in range(labels.shape[1] // EXTRA):
                labels[
                    j, group * EXTRA:(group + 1) * EXTRA, sub * PIECE:(sub + 1) * PIECE
                ] = label_raw[j % 2, sub, j // 2, :, group * PIECE:(group + 1) * PIECE]
    lane = lax.broadcasted_iota(jnp.int32, (WIDTH, 2 * PIECE), 1)
    gap = jnp.where(
        lane < PIECE, lax.broadcasted_iota(jnp.int32, (WIDTH, 2 * PIECE), 0) - lane, -WIDTH
    )
    depth = col_buf.shape[-1]

    def arrive(q):
        j = pairs[2 * q] // ROWS

        @pl.when(q == starts[j])
        def _():
            pltpu.make_async_copy(
                cols.at[0, :, 0, pl.ds(0, PIECE)], col_buf.at[j], col_sem.at[j]
            ).wait()

        row_copy(q, 0, 0).wait()
        row_copy(q, 1, 0).wait()

    def multiply(q):
        return lax.dot_general(
            col_buf[pairs[2 * q] // ROWS].reshape(WIDTH, depth), row_buf[lax.rem(q, 3)],
            (((1,), (1,)), ((), ())),
            preferred_element_type=jnp.float32,
        )

    @pl.when(live > 0)
    def _():
        arrive(0)
        inner_even[...] = multiply(0)

    def step(q, current, following, more):
        @pl.when(q + 2 < live)
        def _():
            start_rows(q + 2)

        if more:
            arrive(q + 1)
            following[...] = multiply(q + 1)
        one = pairs[2 * q]
        two = pairs[2 * q + 1]
        j = one // ROWS
        place_one = lax.rem(one, ROWS)
        place_two = lax.rem(two, ROWS)
        inner = current[...]
        row_part = jnp.concatenate([row_sq[place_one], row_sq[place_two]], axis=1)
        ratio = inner / (
            WEIGHT_ROW * row_part
            + WEIGHT_COL * col_sq[j]
            + WEIGHT_SHARED * inner
            + EPSILON
        )
        offset = jnp.where(one == own_tile, own_offset, -2 * WIDTH)
        value = jnp.where(gap == offset, 0.0, jnp.exp(SHARPNESS * (ratio - 0.5)))
        half = value.astype(jnp.bfloat16)
        spread = jnp.dot(labels[j], half, preferred_element_type=jnp.float32)
        sums = jnp.sum(value, axis=0, keepdims=True)
        tile_buf[one] = half[:, :PIECE]
        tile_copy(one).start()
        total[place_one] += spread[:, :PIECE]
        degree[pl.ds(place_one, 1), :] += sums[:, :PIECE]

        @pl.when(one != two)
        def _():
            tile_buf[two] = half[:, PIECE:]
            tile_copy(two).start()
            total[place_two] += spread[:, PIECE:]
            degree[pl.ds(place_two, 1), :] += sums[:, PIECE:]

    def steps(i, carry):
        for q, current, following in (
            (2 * i, inner_even, inner_odd), (2 * i + 1, inner_odd, inner_even)
        ):
            @pl.when(q + 1 < live)
            def _():
                step(q, current, following, True)

            @pl.when(q + 1 == live)
            def _():
                step(q, current, following, False)

        return carry

    lax.fori_loop(0, (live + 1) // 2, steps, 0)
    for j in range(BLOCKS):
        @pl.when(starts[j] == starts[j + 1])
        def _():
            pltpu.make_async_copy(
                cols.at[0, :, 0, pl.ds(0, PIECE)], col_buf.at[j], col_sem.at[j]
            ).wait()

    split_rows(z, total, keep, send)
    half_rows = ROWS // 2
    for piece in range(half_rows):
        place = lax.rem(z - piece + half_rows, half_rows)
        degree_keep[piece:piece + 1, :] = degree[pl.ds(place, 1), :]
        degree_send[piece:piece + 1, :] = degree[pl.ds(half_rows + place, 1), :]

    def finish(q, carry):
        tile_copy(pairs[2 * q]).wait()

        @pl.when(pairs[2 * q] != pairs[2 * q + 1])
        def _():
            tile_copy(pairs[2 * q + 1]).wait()

        return carry

    lax.fori_loop(0, live, finish, 0)


def build_weights(pairs, meta, starts, rows, cols, row_sq, col_sq):
    smem = pl.BlockSpec(memory_space=pltpu.SMEM)
    vmem = pl.BlockSpec(memory_space=pltpu.VMEM)
    hbm = pl.BlockSpec(memory_space=pl.ANY)
    depth = cols.shape[-1]
    tasks = depth * EXTRA // PIECE
    return pl.pallas_call(
        weights_kernel,
        out_shape=(
            jax.ShapeDtypeStruct((TILES, WIDTH, PIECE), jnp.bfloat16),
            jax.ShapeDtypeStruct((ROWS // 2, tasks, PIECE), jnp.float32),
            jax.ShapeDtypeStruct((ROWS // 2, tasks, PIECE), jnp.bfloat16),
            jax.ShapeDtypeStruct((ROWS // 2, PIECE), jnp.float32),
            jax.ShapeDtypeStruct((ROWS // 2, PIECE), jnp.float32),
        ),
        in_specs=[smem, smem, smem] + [hbm] * ROWS + [hbm, vmem, vmem],
        out_specs=(hbm, vmem, vmem, vmem, vmem),
        scratch_shapes=[
            pltpu.VMEM((BLOCKS, WIDTH // PIECE, PIECE, depth), jnp.bfloat16),
            pltpu.VMEM((3, 2 * PIECE, depth), jnp.bfloat16),
            pltpu.VMEM((TILES, WIDTH, PIECE), jnp.bfloat16),
            pltpu.VMEM((2, 4, 2, EXTRA, depth), jnp.bfloat16),
            pltpu.VMEM((BLOCKS, tasks, WIDTH), jnp.bfloat16),
            pltpu.VMEM((ROWS, tasks, PIECE), jnp.float32),
            pltpu.VMEM((ROWS, PIECE), jnp.float32),
            pltpu.VMEM((WIDTH, 2 * PIECE), jnp.float32),
            pltpu.VMEM((WIDTH, 2 * PIECE), jnp.float32),
            pltpu.SemaphoreType.DMA((BLOCKS,)),
            pltpu.SemaphoreType.DMA((3, 2)),
            pltpu.SemaphoreType.DMA((TILES,)),
            pltpu.SemaphoreType.DMA,
        ],
        compiler_params=pltpu.CompilerParams(vmem_limit_bytes=VMEM_LIMIT),
        cost_estimate=pl.CostEstimate(
            flops=16 * 2 * PIECE * WIDTH * depth,
            bytes_accessed=2 * (ROWS + 16) * PIECE * depth,
            transcendentals=16 * PIECE * WIDTH,
        ),
        name="weights",
    )(pairs, meta, starts, *rows, cols, row_sq, col_sq)


def spread_kernel(pairs, meta, starts, weights, pieces, keep, send, total, tile_buf, tile_sem):
    live = starts[BLOCKS]
    z = meta[3]
    half = ROWS // 2

    def tile_copy(q, side):
        return pltpu.make_async_copy(
            weights.at[pairs[2 * q + side]],
            tile_buf.at[q, :, pl.ds(side * PIECE, PIECE)],
            tile_sem.at[q, side],
        )

    def begin(q, carry):
        tile_copy(q, 0).start()

        @pl.when(pairs[2 * q] != pairs[2 * q + 1])
        def _():
            tile_copy(q, 1).start()

        return carry

    lax.fori_loop(0, live, begin, 0)
    total[...] = jnp.zeros_like(total)

    def add(tile_id, value):
        a = lax.rem(tile_id, ROWS)
        side = a // half
        place = side * half + lax.rem(z - lax.rem(a, half) + half, half)
        total[place] += value

    def pair(q, carry):
        one = pairs[2 * q]
        two = pairs[2 * q + 1]
        tile_copy(q, 0).wait()

        @pl.when(one != two)
        def _():
            tile_copy(q, 1).wait()

        j = one // ROWS
        spread = jnp.dot(
            jnp.concatenate([pieces[j * 4 + sub] for sub in range(WIDTH // PIECE)], axis=1),
            tile_buf[q], preferred_element_type=jnp.float32,
        )
        add(one, spread[:, :PIECE])

        @pl.when(one != two)
        def _():
            add(two, spread[:, PIECE:])

        return carry

    lax.fori_loop(0, live, pair, 0)
    keep[...] = total[:half]
    send[...] = total[half:].astype(jnp.bfloat16)


def spread_rows(pairs, meta, starts, weights, pieces):
    smem = pl.BlockSpec(memory_space=pltpu.SMEM)
    vmem = pl.BlockSpec(memory_space=pltpu.VMEM)
    hbm = pl.BlockSpec(memory_space=pl.ANY)
    tasks = pieces.shape[1]
    return pl.pallas_call(
        spread_kernel,
        out_shape=(
            jax.ShapeDtypeStruct((ROWS // 2, tasks, PIECE), jnp.float32),
            jax.ShapeDtypeStruct((ROWS // 2, tasks, PIECE), jnp.bfloat16),
        ),
        in_specs=[smem, smem, smem, hbm, vmem],
        out_specs=(vmem, vmem),
        scratch_shapes=[
            pltpu.VMEM((ROWS, tasks, PIECE), jnp.float32),
            pltpu.VMEM((TILES // 2, WIDTH, 2 * PIECE), jnp.bfloat16),
            pltpu.SemaphoreType.DMA((TILES // 2, 2)),
        ],
        compiler_params=pltpu.CompilerParams(vmem_limit_bytes=VMEM_LIMIT),
        name="spread",
    )(pairs, meta, starts, weights, pieces)


def swap_cores(value):
    return lax.ppermute(value, "core", [(0, 1), (1, 0)])


def gather_pieces(piece):
    copies = jnp.broadcast_to(piece[None], (ROWS,) + piece.shape)
    return lax.all_to_all(copies, PLANE, 0, 0)


def body(fingerprints, activity, label_mask, pattern, counts):
    y, xh, z, xl, core = [lax.axis_index(axis) for axis in AXES]
    depth = fingerprints.shape[1]
    slots = pattern.shape[1]
    tasks = activity.shape[1]
    extended, seeded = prepare(fingerprints, activity, label_mask)
    cols = lax.all_gather(extended, ("y", "xh", "xl"), axis=0, tiled=True)
    cols = cols.reshape(2, 4, 2, PIECE + EXTRA, depth)

    upward = [fingerprints]
    for step in range(4):
        upward.append(lax.ppermute(upward[-1], "z", [(i, (i + 1) % 8) for i in range(8)]))
    downward = [fingerprints]
    for step in range(3):
        downward.append(lax.ppermute(downward[-1], "z", [(i, (i + 7) % 8) for i in range(8)]))
    rows = upward + [downward[3], downward[2], downward[1]]
    rows = rows + [swap_cores(row) for row in rows]

    squares = jnp.sum(jnp.square(fingerprints.astype(jnp.float32)), axis=1)
    table = jnp.concatenate([counts[:, None], pattern], axis=1).astype(jnp.float32).reshape(-1)
    info = jnp.concatenate([squares, table, jnp.zeros((PIECE - table.size,), jnp.float32)])
    info = jnp.broadcast_to(info[None, None], (ROWS, 8, 2 * PIECE))
    info = lax.all_to_all(info, ("core", "z"), 0, 0)[:, 0]
    away = jnp.arange(8, dtype=jnp.int32)
    nearby = (z - away) % 8
    line_info = info[jnp.concatenate([core * 8 + nearby, (1 - core) * 8 + nearby])]
    row_sq = line_info[:, :PIECE].reshape(ROWS, 1, PIECE)
    squares, rows[4], rows[5] = lax.optimization_barrier((squares, rows[4], rows[5]))
    col_sq = gather_pieces(jnp.broadcast_to(squares[None], (8, PIECE)))[:, 0]
    col_sq = col_sq.reshape(BLOCKS, WIDTH, 1)
    tables = line_info[:, PIECE:PIECE + table.size].reshape(ROWS, 2, slots + 1)
    mine = lax.dynamic_index_in_dim(tables.astype(jnp.int32), y // 2, 1, keepdims=False)

    j = jnp.arange(BLOCKS, dtype=jnp.int32)
    col_block = (z * 4 + (j // 2) * 2 + core) * 2 + j % 2
    hit = (mine[None, :, 1:] == col_block[:, None, None]) & (
        jnp.arange(slots, dtype=jnp.int32)[None, None, :] < mine[None, :, :1]
    )
    live = jnp.any(hit, axis=2)
    flat = live.reshape(TILES).astype(jnp.int32)
    order = jnp.arange(TILES, dtype=jnp.int32)
    before = jnp.sum(jnp.where(order[None, :] < order[:, None], flat[None, :], 0), axis=1)
    counted = jnp.sum(live.astype(jnp.int32), axis=1)
    even = counted + counted % 2
    block_start = jnp.sum(jnp.where(j[None, :] < j[:, None], even[None, :], 0), axis=1)
    block_before = jnp.sum(jnp.where(j[None, :] < j[:, None], counted[None, :], 0), axis=1)
    position = before + jnp.repeat(block_start - block_before, ROWS)
    spot = jnp.arange(TILES + 8, dtype=jnp.int32)
    pairs = jnp.max(
        jnp.where((position[None, :] <= spot[:, None]) & (flat[None, :] > 0), order[None, :], 0),
        axis=1,
    ).astype(jnp.int32)
    starts = (jnp.concatenate([block_start, jnp.sum(even)[None]]) // 2).astype(jnp.int32)
    own_tile = (xl * 2 + y // 2) * ROWS
    own_offset = ((y % 2) * 2 + xh) * PIECE
    meta = jnp.stack([jnp.sum(flat), own_offset, own_tile, z]).astype(jnp.int32)

    weights, keep, send, degree_keep, degree_send = build_weights(
        pairs, meta, starts, rows, cols, row_sq, col_sq
    )
    degree_sum = degree_keep + swap_cores(degree_send)
    high = lax.reduce_precision(degree_sum, 8, 7)
    low = degree_sum - high
    degree_rows = jnp.stack([high, low], axis=1).astype(jnp.bfloat16)
    degree_rows = jnp.concatenate([degree_rows, jnp.zeros((8, 14, PIECE), jnp.bfloat16)], axis=1)

    for iteration in range(ITERS):
        if iteration > 0:
            keep, send = spread_rows(pairs, meta, starts, weights, gathered)
        part = (keep + swap_cores(send).astype(jnp.float32)).astype(jnp.bfloat16)
        if iteration == 0:
            part = jnp.concatenate([part, degree_rows], axis=1)
        parts = lax.all_to_all(part, "z", 0, 0)
        summed = jnp.sum(parts.astype(jnp.float32), axis=0)
        if iteration == 0:
            degree_own = summed[tasks] + summed[tasks + 1]
            summed = summed[:tasks]
        labels = (PROPAGATE * summed / degree_own[None, :] + ANCHOR * seeded).astype(jnp.bfloat16)
        if iteration < ITERS - 1:
            gathered = gather_pieces(labels)
    return labels.T


def solution(mesh):
    split = Mesh(mesh.devices.reshape(SIZES), AXES)
    whole = ("z", "xl", "core", "y", "xh")
    blocks = ("z", "xl", "core")
    placed = (P(whole, None), P(whole, None), P(whole), P(blocks, None), P(blocks))
    return jax.shard_map(
        body, mesh=split, in_specs=placed, out_specs=P(whole, None), check_vma=False
    )
```
